512 devices in a mesh: qa: 16 (over z_hi, y, core), qb: 32 (over x, z_lo).
Axes of the slice: x: 4, y: 4, z: 16 (z_hi: 2, z_lo: 8; z = z_hi * 8 + z_lo), core: 2. Of those that a mesh axis runs over, the one named last changes fastest.
Arguments:
- amplitudes: float32 [16, 32, 16, 128, 128], P('qa', 'qb'), may hold values from -6 to 6
- angles: float32 [2, 23], replicated, may hold values from -3.140625 to 3.140625
- hadamard: int32 [2, 23], replicated, may hold values 0 or 1
- cz_pairs: int32 [2, 14, 2], replicated, may hold values from 0 to 26, as said below
Outputs:
- final_state: float32 [16, 32, 16, 128, 128], P('qa', 'qb')
The draws below stay inside these ranges and needn't reach their ends.
Inputs may be any that keep to these rules, and one draw needn't show every extreme that they name: `cz_pairs`: the two qubits of a pair differ; in each layer the pairs are a random matching of all 27 qubits, and when 27 is odd one qubit is in two pairs.
All inputs are finite; a program needn't handle non-finite values.
Results may differ from the reference program's by a relative error of at most 0.00013.
Values sent between devices are 32-bit elements; how exact they have to be, the bound alone decides.
A program may use at most 64 MiB of HBM per device.

```python
import math
import jax
import jax.numpy as jnp
from jax import lax

XS = 16
M = 128
K = 128
LAYERS = 2
QA_BITS = 4
QB_BITS = 5
XBITS = 4
MBITS = 7
KBITS = 7
QROT = 23
QUBITS = 27
PAIRS = 14
N_QA = 16
N_QB = 32


def draw_cz_pairs(key, part):
    key = jax.random.fold_in(key, 11)
    layer_keys = jax.random.split(key, LAYERS)

    def one_layer(layer_key):
        ordering = jax.random.permutation(layer_key, QUBITS).astype(jnp.int32)
        extended = jnp.concatenate([ordering, ordering[0:1]])
        return extended[0:2 * PAIRS].reshape(PAIRS, 2)
    return jax.vmap(one_layer)(layer_keys).astype(jnp.int32)


def touch_ends(values, own_key, smallest, largest):
    longest = values.shape.index(max(values.shape))
    spots = []
    for shift in (0, 1):
        where = [jax.random.randint(jax.random.fold_in(own_key, axis), (), 0, length) for axis, length in enumerate(values.shape)]
        where[longest] = (where[longest] + shift) % values.shape[longest]
        spots.append(tuple(where))
    return values.at[spots[0]].set(smallest).at[spots[1]].set(largest)


def steps_of(own_key, extent, pieces, smallest, high):
    level, own = 1.0, jax.random.fold_in(own_key, 6)
    for dim, parts in pieces:
        draws = jnp.exp(jax.random.uniform(jax.random.fold_in(own, dim), (parts,), jnp.float32, smallest / len(pieces), high / len(pieces)))
        level = level * jnp.repeat(draws, extent[dim] // parts).reshape([-1 if axis == dim else 1 for axis in range(len(extent))])
    return level


def gaussian(stream_key, shape, spread, reach, cuts=(), kind=jnp.bfloat16):
    level = steps_of(stream_key, shape, cuts, -0.22, 0.18) if cuts else 1.0
    entries = jax.random.normal(stream_key, shape, jnp.float32) * spread * level
    return jnp.minimum(jnp.maximum(entries, -reach), reach).astype(kind)


def setup_inputs(seed: int = 0) -> dict:
    seeds = jax.random.split(jax.random.key(seed), 5)
    amplitudes = gaussian(seeds[0], (N_QA, N_QB, XS, M, K), 1.0, 6.0, ((0, 16), (1, 32)), jnp.float32)
    angles = jnp.clip(jax.random.uniform(seeds[1], (LAYERS, QROT), jnp.float32, -3.140625, 3.140625), -3.140625, 3.140625)
    hadamard = touch_ends((jax.random.randint(seeds[2], (LAYERS, QROT), 0, 2) < 1).astype(jnp.int32), jax.random.fold_in(seeds[2], 1), 0, 1)
    cz_pairs = draw_cz_pairs(jax.random.fold_in(seeds[4], 71), 0)
    return dict(amplitudes=amplitudes, angles=angles, hadamard=hadamard, cz_pairs=cz_pairs)


HIGHEST_PRECISION = lax.Precision.HIGHEST

def gate_of(angle, flag):
    cos_part = jnp.cos(angle)
    sin_part = jnp.sin(angle)
    root = math.sqrt(0.5)
    weight = flag.astype(jnp.float32)
    rotate = jnp.stack([jnp.stack([cos_part, -sin_part]), jnp.stack([sin_part, cos_part])])
    mixing = jnp.stack([jnp.stack([1.0 - weight + weight * root, weight * root]), jnp.stack([weight * root, 1.0 - weight - weight * root])])
    return jnp.dot(rotate, mixing, precision=HIGHEST_PRECISION)

def group_matrix(angle_row, flag_row):
    matrix = jnp.ones((1, 1), jnp.float32)
    for position in range(angle_row.shape[0]):
        matrix = jnp.kron(matrix, gate_of(angle_row[position], flag_row[position]))
    return matrix

def bits_of(values, count):
    powers = 2 ** (count - 1 - jnp.arange(count, dtype=jnp.int32))
    return (values[:, None] // powers[None, :] % 2).astype(jnp.float32)

def placed(bit_block, offset, total):
    rows = bit_block.shape[0]
    return jnp.concatenate([jnp.zeros((rows, offset), jnp.float32), bit_block, jnp.zeros((rows, total - offset - bit_block.shape[1]), jnp.float32)], axis=1)

def pair_matrix(layer_pairs, total):
    qubit_ids = jnp.arange(total, dtype=jnp.int32)
    first_one = (layer_pairs[:, 0:1] == qubit_ids[None, :]).astype(jnp.float32)
    second_one = (layer_pairs[:, 1:2] == qubit_ids[None, :]).astype(jnp.float32)
    counts = jnp.dot(first_one.T, second_one, precision=HIGHEST_PRECISION)
    return counts + counts.T

def exact_dot(left, right):
    return jnp.dot(left, right, precision=HIGHEST_PRECISION)

def sign_field(coarse_bits, row_bits, col_bits, coupling):
    coarse_c = exact_dot(coarse_bits, coupling)
    row_c = exact_dot(row_bits, coupling)
    self_coarse = lax.optimization_barrier(jnp.sum(coarse_c * coarse_bits, axis=1))
    self_rows = lax.optimization_barrier(jnp.sum(row_c * row_bits, axis=1))
    self_cols = lax.optimization_barrier(jnp.sum(exact_dot(col_bits, coupling) * col_bits, axis=1))
    coarse_rows = 2.0 * exact_dot(coarse_c, row_bits.T)
    coarse_cols = 2.0 * exact_dot(coarse_c, col_bits.T)
    rows_cols = 2.0 * exact_dot(row_c, col_bits.T)
    total = self_coarse[:, None, None] + self_rows[None, :, None] + self_cols[None, None, :] + coarse_rows[:, :, None] + coarse_cols[:, None, :] + rows_cols[None, :, :]
    return 1.0 - jnp.mod(total, 4.0)

def reference(amplitudes, angles, hadamard, cz_pairs):
    rot_b = QA_BITS
    rot_m = QA_BITS + QB_BITS
    rot_k = rot_m + MBITS
    coarse_count = QA_BITS + QB_BITS + XBITS
    coarse_bits = placed(bits_of(jnp.arange(N_QA * N_QB * XS, dtype=jnp.int32), coarse_count), 0, QUBITS)
    row_bits = placed(bits_of(jnp.arange(M, dtype=jnp.int32), MBITS), coarse_count, QUBITS)
    col_bits = placed(bits_of(jnp.arange(K, dtype=jnp.int32), KBITS), coarse_count + MBITS, QUBITS)
    current = amplitudes
    for layer_no in range(LAYERS):
        angle_row = angles[layer_no]
        flag_row = hadamard[layer_no]
        gate_a = group_matrix(angle_row[0:rot_b], flag_row[0:rot_b])
        gate_b = group_matrix(angle_row[rot_b:rot_m], flag_row[rot_b:rot_m])
        gate_m = group_matrix(angle_row[rot_m:rot_k], flag_row[rot_m:rot_k])
        gate_k = group_matrix(angle_row[rot_k:QROT], flag_row[rot_k:QROT])
        current = jnp.einsum('ij,jbxmk->ibxmk', gate_a, current, precision=HIGHEST_PRECISION)
        current = jnp.einsum('ij,ajxmk->aixmk', gate_b, current, precision=HIGHEST_PRECISION)
        current = jnp.einsum('ij,abxjk->abxik', gate_m, current, precision=HIGHEST_PRECISION)
        current = jnp.einsum('abxmj,ij->abxmi', current, gate_k, precision=HIGHEST_PRECISION)
        signs = sign_field(coarse_bits, row_bits, col_bits, pair_matrix(cz_pairs[layer_no], QUBITS))
        current = current * signs.reshape(current.shape)
    return jnp.transpose(current, (2, 1, 0, 3, 4))
```

```python
import functools
import math

import jax
import jax.numpy as jnp
from jax import lax
from jax.experimental import pallas as pl
from jax.experimental.pallas import tpu as pltpu
from jax.sharding import PartitionSpec as P

MESH = pl.DeviceIdType.MESH
F32 = jnp.float32
BF16 = jnp.bfloat16

Z_HALVES = 2
X_CHIPS = 4


def gate_entries(angles, hadamard):
    layers, count = angles.shape
    shape = (layers, 4, count)
    entry = lax.broadcasted_iota(jnp.int32, shape, 1)
    angle = jnp.broadcast_to(angles[:, None, :], shape)
    weight = jnp.broadcast_to(hadamard[:, None, :], shape).astype(F32)
    cos_part, sin_part = jnp.cos(angle), jnp.sin(angle)
    root = math.sqrt(0.5)
    upper = entry < 2
    left = entry % 2 == 0
    near = jnp.where(upper, cos_part, sin_part)
    far = jnp.where(upper, -sin_part, cos_part)
    mix_near = jnp.where(left, 1.0 - weight + weight * root, weight * root)
    mix_far = jnp.where(left, weight * root, 1.0 - weight - weight * root)
    return near * mix_near + far * mix_far


def split(value):
    high = value.astype(BF16)
    return high, (value - high.astype(F32)).astype(BF16)


def dot3(left, right):
    dot = functools.partial(jnp.dot, preferred_element_type=F32)
    return dot(left[0], right[0]) + (dot(left[0], right[1]) + dot(left[1], right[0]))


def log2(value):
    return value.bit_length() - 1


def kernel(
    sizes,
    gates, pairs, amp, out,
    send_z, recv_z, send_p, recv_p, send_b, recv_b,
    gk, gm, gab, sign_mid, sign_end, mid, send_sem, recv_sem,
):
    zh, zl, xc, yc, halves, ex, kk = sizes
    nz, np_, nb, na = zh * zl, xc * yc, xc * zl, zh * yc
    mm = halves * zl * ex * xc
    nab = na * nb
    bits_a, bits_b, bits_x, bits_m, bits_k = log2(na), log2(nb), log2(na), log2(mm), log2(kk)
    qubits = bits_a + bits_b + bits_x + bits_m + bits_k
    shift_m = bits_k
    shift_x = shift_m + bits_m
    shift_b = shift_x + bits_x
    shift_a = shift_b + bits_b
    rot_m = bits_a + bits_b
    rot_k = rot_m + bits_m
    rows_p = ex * zh * zl
    rows_b = ex * na
    sub = ex * xc

    me_a, me_b = lax.axis_index("qa"), lax.axis_index("qb")
    my_zh, my_yc = lax.div(me_a, yc), lax.rem(me_a, yc)
    my_x, my_zl = lax.div(me_b, zl), lax.rem(me_b, zl)
    my_z = my_zh * zl + my_zl
    my_p = my_x * yc + my_yc

    def either_way(step, count):
        odd = lax.rem(step, 2)
        half = lax.div(step + 1, 2)
        return odd * half + (1 - odd) * (count - half)

    def at_z(step):
        z = lax.rem(my_z + either_way(step, nz), nz)
        return z, (lax.div(z, zl) * yc + my_yc, my_x * zl + lax.rem(z, zl))

    def at_p(step):
        p = lax.rem(my_p + step, np_)
        return p, (my_zh * yc + lax.rem(p, yc), lax.div(p, yc) * zl + my_zl)

    def at_b(step):
        b = lax.rem(my_b_start + step, nb)
        return b, (me_a, b)

    my_b_start = me_b

    barrier = pltpu.get_barrier_semaphore()
    for place, count in ((at_z, nz), (at_p, np_), (at_b, nb)):
        @pl.loop(1, count)
        def _(step, place=place):
            pl.semaphore_signal(barrier, inc=1, device_id=place(step)[1], device_id_type=MESH)

    def entry(layer, qubit, out_one, in_one):
        value = lambda number: gates[layer, number, qubit]
        return jnp.where(
            out_one,
            jnp.where(in_one, value(3), value(2)),
            jnp.where(in_one, value(1), value(0)),
        )

    def matrix(layer, out_index, in_index, qubits_and_bits):
        result = None
        for qubit, out_bit, in_bit in qubits_and_bits:
            factor = entry(
                layer, qubit, (out_index & (1 << out_bit)) != 0, (in_index & (1 << in_bit)) != 0
            )
            result = factor if result is None else result * factor
        return result

    def signs(layer, index):
        odd = jnp.zeros(index.shape, jnp.int32)
        for pair in range(pairs.shape[1]):
            mask = jnp.left_shift(1, qubits - 1 - pairs[layer, pair, 0]) | jnp.left_shift(
                1, qubits - 1 - pairs[layer, pair, 1]
            )
            odd = odd ^ jnp.where((index & mask) == mask, 1, 0)
        return 1.0 - 2.0 * odd.astype(F32)

    def build_k(layer):
        rows = lax.broadcasted_iota(jnp.int32, (kk, kk), 0)
        cols = lax.broadcasted_iota(jnp.int32, (kk, kk), 1)
        bits = [(rot_k + n, bits_k - 1 - n, bits_k - 1 - n) for n in range(bits_k)]
        gk[layer, 0], gk[layer, 1] = split(matrix(layer, cols, rows, bits))

    bits_zl, bits_xc, bits_ex, bits_h = log2(zl), log2(xc), log2(ex), log2(halves)

    def build_m(layer):
        rows = lax.broadcasted_iota(jnp.int32, (mm, mm), 0)
        cols = lax.broadcasted_iota(jnp.int32, (mm, mm), 1)
        natural = [bits_m - 1 - n for n in range(bits_m)]
        if layer == 0:
            in_bits = natural
        else:
            in_bits = (
                natural[:bits_h]
                + [bits_zl - 1 - n for n in range(bits_zl)]
                + [bits_zl + bits_xc + bits_ex - 1 - n for n in range(bits_ex)]
                + [bits_zl + bits_xc - 1 - n for n in range(bits_xc)]
            )
        bits = [(rot_m + n, natural[n], in_bits[n]) for n in range(bits_m)]
        gm[layer, 0], gm[layer, 1] = split(matrix(layer, rows, cols, bits))

    bits_yc, bits_zh = log2(yc), log2(zh)

    def mid_bits():
        a_bits = [bits_zl + bits_zh - 1 - n for n in range(bits_zh)]
        a_bits += [bits_zl + bits_zh + bits_yc - 1 - n for n in range(bits_yc)]
        b_bits = [bits_zl + bits_zh + bits_yc + bits_xc - 1 - n for n in range(bits_xc)]
        b_bits += [bits_zl - 1 - n for n in range(bits_zl)]
        return a_bits + b_bits

    tile = min(nab, 64)

    def build_ab(layer):
        mids = mid_bits()
        if layer == 0:
            outs = mids
        else:
            outs = [bits_a - 1 - n for n in range(bits_a)]
            outs += [bits_a + bits_b - 1 - n for n in range(bits_b)]
        bits = [(n, outs[n], mids[n]) for n in range(bits_a + bits_b)]

        @pl.loop(0, nab // tile)
        def _(step):
            start = pl.multiple_of(step * tile, tile)
            rows = lax.broadcasted_iota(jnp.int32, (tile, nab), 0) + start
            cols = lax.broadcasted_iota(jnp.int32, (tile, nab), 1)
            high, low = split(matrix(layer, rows, cols, bits))
            gab[layer, 0, pl.ds(start, tile), :] = high
            gab[layer, 1, pl.ds(start, tile), :] = low

    sign_tile = min(nab, 128)

    def build_sign_mid():
        mids = mid_bits()
        per = nab // sign_tile

        @pl.loop(0, halves * ex * per)
        def _(step):
            part, start = lax.div(step, per), pl.multiple_of(lax.rem(step, per) * sign_tile, sign_tile)
            half, extra = lax.div(part, ex), lax.rem(part, ex)
            rows = lax.broadcasted_iota(jnp.int32, (sign_tile, kk), 0) + start
            cols = lax.broadcasted_iota(jnp.int32, (sign_tile, kk), 1)
            index = cols
            for n in range(bits_a + bits_b):
                index = index | (((rows >> mids[n]) & 1) << (qubits - 1 - n))
            m = ((half * zl + my_zl) * ex + extra) * xc + my_x
            index = index + (m * (1 << shift_m) + me_a * (1 << shift_x))
            sign_mid[half, pl.ds(start, sign_tile), pl.ds(pl.multiple_of(extra * kk, kk), kk)] = signs(0, index)

    def build_sign_end():
        @pl.loop(0, na)
        def _(a):
            rows = lax.broadcasted_iota(jnp.int32, (mm, kk), 0)
            cols = lax.broadcasted_iota(jnp.int32, (mm, kk), 1)
            index = cols + rows * (1 << shift_m)
            index = index + (me_a * (1 << shift_x) + me_b * (1 << shift_b) + a * (1 << shift_a))
            sign_end[a] = signs(1, index)

    build_k(0)
    build_m(0)
    together = 4

    @pl.loop(0, na // together)
    def _(step):
        first = step * together
        block = amp[pl.ds(first, together)].reshape(together * mm, kk)
        block = dot3(split(block), (gk[0, 0], gk[0, 1]))
        matrix_m = (gm[0, 0], gm[0, 1])
        for n in range(together):
            done = dot3(matrix_m, split(block[n * mm : (n + 1) * mm]))
            done = done.reshape(halves, zl, sub, kk)
            x = first + n
            send_z[:, pl.ds(lax.div(x, yc) * zl, zl), lax.rem(x, yc)] = done

    pl.semaphore_wait(barrier, nz + np_ + nb - 3)

    def send_all(stage, half, count, place, mine, source, target):
        @pl.loop(1, count)
        def _(step):
            number, device = place(step)
            pltpu.make_async_remote_copy(
                src_ref=source.at[half, number],
                dst_ref=target.at[half, mine],
                send_sem=send_sem.at[stage, half],
                recv_sem=recv_sem.at[stage, half],
                device_id=device,
                device_id_type=MESH,
            ).start()

        pltpu.make_async_copy(
            source.at[half, mine], target.at[half, mine], recv_sem.at[stage, half]
        ).start()

    def wait_all(stage, half, target):
        pltpu.make_async_copy(target.at[half], target.at[half], recv_sem.at[stage, half]).wait()

    def wait_sent(stage, half, count, source):
        part = source.at[half, pl.ds(0, count - 1)]
        pltpu.make_async_copy(part, part, send_sem.at[stage, half]).wait()

    for half in range(halves):
        send_all(0, half, nz, at_z, my_z, send_z, recv_z)

    build_ab(0)
    build_ab(1)
    build_sign_mid()

    @pl.loop(0, halves)
    def _(half):
        wait_all(0, half, recv_z)

        @pl.loop(0, yc)
        def _(xr):
            for z_half in range(zh):
                for low in range(sub):
                    rows = recv_z[half, pl.ds(z_half * zl, zl), xr, low, :]
                    extra, x = low // xc, low % xc
                    send_p[half, x * yc + xr, pl.ds((extra * zh + z_half) * zl, zl), :] = rows

        send_all(1, half, np_, at_p, my_p, send_p, recv_p)
        wait_all(1, half, recv_p)
        parts = []
        for extra in range(ex):
            part = recv_p[half, :, pl.ds(extra * zh * zl, zh * zl), :]
            parts.append(part.reshape(nab, kk))
        high, low = split(jnp.concatenate(parts, axis=1))
        mid[0, 0] = high
        mid[0, 1] = low
        mid_tile = min(nab, 128)

        @pl.loop(0, nab // mid_tile)
        def _(step):
            start = pl.multiple_of(step * mid_tile, mid_tile)
            left = (gab[0, 0, pl.ds(start, mid_tile), :], gab[0, 1, pl.ds(start, mid_tile), :])
            value = dot3(left, (mid[0, 0], mid[0, 1])) * sign_mid[half, pl.ds(start, mid_tile), :]
            high, low = split(value)
            mid[1, 0, pl.ds(start, mid_tile), :] = high
            mid[1, 1, pl.ds(start, mid_tile), :] = low

        @pl.loop(0, nab // mid_tile)
        def _(step):
            start = pl.multiple_of(step * mid_tile, mid_tile)
            left = (gab[1, 0, pl.ds(start, mid_tile), :], gab[1, 1, pl.ds(start, mid_tile), :])
            value = dot3(left, (mid[1, 0], mid[1, 1]))
            places = mid_tile // na
            for extra in range(ex):
                part = value[:, extra * kk : (extra + 1) * kk].reshape(places, na, kk)
                send_b[half, pl.ds(step * places, places), pl.ds(extra * na, na), :] = part

        send_all(2, half, nb, at_b, me_b, send_b, recv_b)

    build_k(1)
    build_m(1)
    build_sign_end()
    for half in range(halves):
        wait_all(2, half, recv_b)

    @pl.loop(0, na)
    def _(a):
        parts = []
        for half in range(halves):
            for extra in range(ex):
                for x in range(xc):
                    parts.append(recv_b[half, pl.ds(x * zl, zl), extra * na + a, :])
        block = jnp.concatenate(parts, axis=0)
        block = dot3(split(block), (gk[1, 0], gk[1, 1]))
        block = dot3((gm[1, 0], gm[1, 1]), split(block))
        out[a] = block * sign_end[a]

    for half in range(halves):
        wait_sent(0, half, nz, send_z)
        wait_sent(1, half, np_, send_p)
        wait_sent(2, half, nb, send_b)


def per_device(amplitudes, angles, hadamard, cz_pairs):
    count_a, count_b = lax.axis_size("qa"), lax.axis_size("qb")
    x_total, mm, kk = amplitudes.shape[2:]
    zh, xc = Z_HALVES, X_CHIPS
    yc, zl = count_a // zh, count_b // xc
    halves = 2
    ex = mm // (halves * zl * xc)
    sizes = (zh, zl, xc, yc, halves, ex, kk)
    nab = count_a * count_b
    vmem = pl.BlockSpec(memory_space=pltpu.VMEM)
    smem = pl.BlockSpec(memory_space=pltpu.SMEM)
    shape_z = (halves, zh * zl, yc, ex * xc, kk)
    shape_p = (halves, xc * yc, ex * zh * zl, kk)
    shape_b = (halves, xc * zl, ex * count_a, kk)
    result = pl.pallas_call(
        functools.partial(kernel, sizes),
        out_shape=jax.ShapeDtypeStruct((count_a, mm, kk), F32),
        in_specs=[smem, smem, vmem],
        out_specs=vmem,
        scratch_shapes=[
            pltpu.VMEM(shape_z, F32),
            pltpu.VMEM(shape_z, F32),
            pltpu.VMEM(shape_p, F32),
            pltpu.VMEM(shape_p, F32),
            pltpu.VMEM(shape_b, F32),
            pltpu.VMEM(shape_b, F32),
            pltpu.VMEM((2, 2, kk, kk), BF16),
            pltpu.VMEM((2, 2, mm, mm), BF16),
            pltpu.VMEM((2, 2, nab, nab), BF16),
            pltpu.VMEM((halves, nab, ex * kk), F32),
            pltpu.VMEM((count_a, mm, kk), F32),
            pltpu.VMEM((2, 2, nab, ex * kk), BF16),
            pltpu.SemaphoreType.DMA((3, halves)),
            pltpu.SemaphoreType.DMA((3, halves)),
        ],
        compiler_params=pltpu.CompilerParams(
            collective_id=0, has_side_effects=True, vmem_limit_bytes=40 * 2**20
        ),
    )(gate_entries(angles, hadamard), cz_pairs, amplitudes.reshape(x_total, mm, kk))
    return result.reshape(1, 1, count_a, mm, kk)


def solution(mesh):
    return jax.shard_map(
        per_device,
        mesh=mesh,
        in_specs=(P("qa", "qb", None, None, None), P(), P(), P()),
        out_specs=P("qa", "qb", None, None, None),
        check_vma=False,
    )
```

```python
import functools
import math

import jax
import jax.numpy as jnp
from jax import lax
from jax.experimental import pallas as pl
from jax.experimental.pallas import tpu as pltpu
from jax.sharding import PartitionSpec as P

MESH = pl.DeviceIdType.MESH
F32 = jnp.float32
BF16 = jnp.bfloat16
IN_SPACE = pltpu.HBM

Z_HALVES = 2
X_CHIPS = 4


def gate_entries(angle, flag):
    cos_part, sin_part = jnp.cos(angle), jnp.sin(angle)
    weight = flag.astype(F32)
    root = math.sqrt(0.5)
    stay, mix, turn = 1.0 - weight + weight * root, weight * root, 1.0 - weight - weight * root
    return (
        cos_part * stay - sin_part * mix,
        cos_part * mix - sin_part * turn,
        sin_part * stay + cos_part * mix,
        sin_part * mix + cos_part * turn,
    )


def split(value):
    high = value.astype(BF16)
    return high, (value - high.astype(F32)).astype(BF16)


def dot3(left, right):
    dot = functools.partial(jnp.dot, preferred_element_type=F32)
    return dot(left[0], right[0]) + (dot(left[0], right[1]) + dot(left[1], right[0]))


def log2(value):
    return value.bit_length() - 1


def kernel(
    sizes,
    amp_in, angles_in, flags_in, pairs_in, out,
    send_z, recv_z, send_p, recv_p, send_b, recv_b,
    gk, gm, gm_end, gab, sign_mid, sign_end, mid,
    amp, angles, flags, entries, gates, pairs, send_sem, recv_sem, load_sem,
):
    zh, zl, xc, yc, halves, ex, kk = sizes
    nz, np_, nb, na = zh * zl, xc * yc, xc * zl, zh * yc
    mm = halves * zl * ex * xc
    nab = na * nb
    bits_a, bits_b, bits_x, bits_m, bits_k = log2(na), log2(nb), log2(na), log2(mm), log2(kk)
    qubits = bits_a + bits_b + bits_x + bits_m + bits_k
    shift_m = bits_k
    shift_x = shift_m + bits_m
    shift_b = shift_x + bits_x
    shift_a = shift_b + bits_b
    rot_m = bits_a + bits_b
    rot_k = rot_m + bits_m
    sub = ex * xc
    together = 4
    steps = yc // together if yc > together else 1
    together = yc // steps

    me_a, me_b = lax.axis_index("qa"), lax.axis_index("qb")
    my_zh, my_yc = lax.div(me_a, yc), lax.rem(me_a, yc)
    my_x, my_zl = lax.div(me_b, zl), lax.rem(me_b, zl)
    my_z = my_zh * zl + my_zl
    my_p = my_x * yc + my_yc

    def at_z(other, step):
        z_half = lax.rem(my_zh + other, zh)
        z_low = lax.rem(my_zl + step, zl)
        return z_half * zl + z_low, (z_half * yc + my_yc, my_x * zl + z_low)

    def at_p(step):
        p = lax.rem(my_p + step, np_)
        return p, (my_zh * yc + lax.rem(p, yc), lax.div(p, yc) * zl + my_zl)

    run = zl // 2

    def at_b(other, step):
        side = lax.rem(lax.div(my_zl, run) + other, 2)
        place = side * run + lax.rem(my_zl + step, run)
        b = lax.rem(my_x + lax.div(step, run), xc) * zl + place
        return b, (me_a, b)

    def load(number, source, target):
        return pltpu.make_async_copy(source, target, load_sem.at[number])

    small = [load(0, angles_in, angles), load(1, flags_in, flags), load(2, pairs_in, pairs)]
    for copy in small:
        copy.start()

    def amp_part(number):
        z_half = lax.rem(my_zh + 1 + number // steps, zh)
        first = z_half * yc + number % steps * together
        part = pl.ds(first, together)
        return z_half, first, load(3 + number, amp_in.at[part], amp.at[part])

    for number in range(zh * steps):
        amp_part(number)[2].start()

    barrier = pltpu.get_barrier_semaphore()

    def signal(device):
        pl.semaphore_signal(barrier, inc=1, device_id=device, device_id_type=MESH)

    for other in (1, 0):
        pl.loop(1 - other, zl)(lambda step, other=other: signal(at_z(other, step)[1]))
    for other in (1, 0):
        pl.loop(1 - other, nb // 2)(lambda step, other=other: signal(at_b(other, step)[1]))
    pl.loop(1, np_)(lambda step: signal(at_p(step)[1]))

    small[0].wait()
    small[1].wait()
    for number, value in enumerate(gate_entries(angles[...], flags[...])):
        entries[number] = value
    to_scalars = load(0, entries, gates)
    to_scalars.start()
    small[2].wait()
    to_scalars.wait()

    def entry(layer, qubit, out_one, in_one):
        value = lambda number: gates[number, layer, qubit]
        return jnp.where(
            out_one,
            jnp.where(in_one, value(3), value(2)),
            jnp.where(in_one, value(1), value(0)),
        )

    def matrix(layer, out_index, in_index, qubits_and_bits):
        result = None
        for qubit, out_bit, in_bit in qubits_and_bits:
            factor = entry(
                layer, qubit, (out_index & (1 << out_bit)) != 0, (in_index & (1 << in_bit)) != 0
            )
            result = factor if result is None else result * factor
        return result

    def signs(layer, index):
        odd = jnp.zeros(index.shape, jnp.int32)
        for pair in range(pairs.shape[2]):
            mask = jnp.left_shift(1, qubits - 1 - pairs[layer, 0, pair]) | jnp.left_shift(
                1, qubits - 1 - pairs[layer, 1, pair]
            )
            odd = odd ^ jnp.where((index & mask) == mask, 1, 0)
        return 1.0 - 2.0 * odd.astype(F32)

    def build_k(layer):
        rows = lax.broadcasted_iota(jnp.int32, (kk, kk), 0)
        cols = lax.broadcasted_iota(jnp.int32, (kk, kk), 1)
        bits = [(rot_k + n, bits_k - 1 - n, bits_k - 1 - n) for n in range(bits_k)]
        gk[layer, 0], gk[layer, 1] = split(matrix(layer, cols, rows, bits))

    bits_zl, bits_xc, bits_ex, bits_h = log2(zl), log2(xc), log2(ex), log2(halves)

    natural = [bits_m - 1 - n for n in range(bits_m)]

    def build_m():
        rows = lax.broadcasted_iota(jnp.int32, (mm, mm), 0)
        cols = lax.broadcasted_iota(jnp.int32, (mm, mm), 1)
        bits = [(rot_m + n, natural[n], natural[n]) for n in range(bits_m)]
        gm[0], gm[1] = split(matrix(0, rows, cols, bits))

    def build_m_end():
        columns = mm // halves
        rows = lax.broadcasted_iota(jnp.int32, (mm, columns), 0)
        in_bits = (
            natural[:bits_h]
            + [bits_zl - 1 - n for n in range(bits_zl)]
            + [bits_zl + bits_xc + bits_ex - 1 - n for n in range(bits_ex)]
            + [bits_zl + bits_xc - 1 - n for n in range(bits_xc)]
        )
        bits = [(rot_m + n, natural[n], in_bits[n]) for n in range(bits_m)]
        for half in range(halves):
            cols = lax.broadcasted_iota(jnp.int32, (mm, columns), 1) + half * columns
            gm_end[half, 0], gm_end[half, 1] = split(matrix(1, rows, cols, bits))

    bits_yc, bits_zh = log2(yc), log2(zh)

    def mid_bits():
        a_bits = [bits_zl + bits_zh - 1 - n for n in range(bits_zh)]
        a_bits += [bits_zl + bits_zh + bits_yc - 1 - n for n in range(bits_yc)]
        b_bits = [bits_zl + bits_zh + bits_yc + bits_xc - 1 - n for n in range(bits_xc)]
        b_bits += [bits_zl - 1 - n for n in range(bits_zl)]
        return a_bits + b_bits

    tile = min(nab, 64)

    def build_ab(layer):
        mids = mid_bits()
        if layer == 0:
            outs = mids
        else:
            outs = [bits_a - 1 - n for n in range(bits_a)]
            outs += [bits_a + bits_b - 1 - n for n in range(bits_b)]
        bits = [(n, outs[n], mids[n]) for n in range(bits_a + bits_b)]

        @pl.loop(0, nab // tile)
        def _(step):
            start = pl.multiple_of(step * tile, tile)
            rows = lax.broadcasted_iota(jnp.int32, (tile, nab), 0) + start
            cols = lax.broadcasted_iota(jnp.int32, (tile, nab), 1)
            high, low = split(matrix(layer, rows, cols, bits))
            gab[layer, 0, pl.ds(start, tile), :] = high
            gab[layer, 1, pl.ds(start, tile), :] = low

    sign_tile = min(nab, 128)

    def build_sign_mid():
        mids = mid_bits()
        per = nab // sign_tile

        @pl.loop(0, halves * ex * per)
        def _(step):
            part, start = lax.div(step, per), pl.multiple_of(lax.rem(step, per) * sign_tile, sign_tile)
            half, extra = lax.div(part, ex), lax.rem(part, ex)
            rows = lax.broadcasted_iota(jnp.int32, (sign_tile, kk), 0) + start
            cols = lax.broadcasted_iota(jnp.int32, (sign_tile, kk), 1)
            index = cols
            for n in range(bits_a + bits_b):
                index = index | (((rows >> mids[n]) & 1) << (qubits - 1 - n))
            m = ((half * zl + my_zl) * ex + extra) * xc + my_x
            index = index + (m * (1 << shift_m) + me_a * (1 << shift_x))
            sign_mid[half, pl.ds(start, sign_tile), pl.ds(pl.multiple_of(extra * kk, kk), kk)] = signs(0, index)

    def build_sign_end():
        @pl.loop(0, na)
        def _(a):
            rows = lax.broadcasted_iota(jnp.int32, (mm, kk), 0)
            cols = lax.broadcasted_iota(jnp.int32, (mm, kk), 1)
            index = cols + rows * (1 << shift_m)
            index = index + (me_a * (1 << shift_x) + me_b * (1 << shift_b) + a * (1 << shift_a))
            sign_end[a] = signs(1, index)

    def beside(value, rows):
        parts = [value[n * rows : (n + 1) * rows] for n in range(together)]
        return jnp.concatenate(parts, axis=1)

    def layer_0(number):
        z_half, first, copy = amp_part(number)
        copy.wait()
        block = amp[pl.ds(first, together)].reshape(together * mm, kk)
        block = dot3(split(block), (gk[0, 0], gk[0, 1]))
        high, low = split(block)
        block = dot3((gm[0], gm[1]), (beside(high, mm), beside(low, mm)))
        for n in range(together):
            done = block[:, n * kk : (n + 1) * kk].reshape(halves, zl, sub, kk)
            send_z[:, pl.ds(z_half * zl, zl), number % steps * together + n] = done

    def send(source, target, sems, device):
        pltpu.make_async_remote_copy(
            src_ref=source,
            dst_ref=target,
            send_sem=send_sem.at[sems],
            recv_sem=recv_sem.at[sems],
            device_id=device,
            device_id_type=MESH,
        ).start()

    def keep(source, target, sems):
        pltpu.make_async_copy(source, target, recv_sem.at[sems]).start()

    def wait_all(target, sems):
        pltpu.make_async_copy(target, target, recv_sem.at[sems]).wait()

    def wait_sent(part, sems):
        pltpu.make_async_copy(part, part, send_sem.at[sems]).wait()

    def send_z_part(half, other):
        @pl.loop(1 - other, zl)
        def _(step):
            number, device = at_z(other, step)
            send(send_z.at[half, number], recv_z.at[half, my_z], half, device)

    def keep_z(half):
        keep(send_z.at[half, my_z], recv_z.at[half, my_z], half)

    def send_p_half(half):
        @pl.loop(1, np_)
        def _(step):
            number, device = at_p(step)
            send(send_p.at[half, number], recv_p.at[half, my_p], 2 + half, device)

        keep(send_p.at[half, my_p], recv_p.at[half, my_p], 2 + half)

    def b_part(ref, half, number, group):
        return ref.at[half, number] if half == 0 else ref.at[half, number, group]

    def b_parts(half):
        return [(0, 4)] if half == 0 else [(group, 5 + group) for group in range(zh)]

    def send_b_half(half):
        for group, sems in b_parts(half):
            for other in (1, 0):
                @pl.loop(1 - other, nb // 2)
                def _(step):
                    number, device = at_b(other, step)
                    send(b_part(send_b, half, number, group), b_part(recv_b, half, me_b, group), sems, device)

            keep(b_part(send_b, half, me_b, group), b_part(recv_b, half, me_b, group), sems)

    build_k(0)
    build_m()
    for number in range(steps):
        layer_0(number)
    pl.semaphore_wait(barrier, nz + np_ + nb - 3)
    send_z_part(0, 1)
    for number in range(steps, zh * steps):
        layer_0(number)
    send_z_part(0, 0)
    keep_z(0)
    send_z_part(1, 1)
    send_z_part(1, 0)
    keep_z(1)

    build_ab(0)
    build_ab(1)
    build_sign_mid()
    mid_tile = min(nab, 128)

    def middle(half):
        wait_all(recv_z.at[half], half)

        @pl.loop(0, yc)
        def _(xr):
            for z_half in range(zh):
                for low in range(sub):
                    rows = recv_z[half, pl.ds(z_half * zl, zl), xr, low, :]
                    extra, x = low // xc, low % xc
                    send_p[half, x * yc + xr, pl.ds((extra * zh + z_half) * zl, zl), :] = rows

        send_p_half(half)
        wait_all(recv_p.at[half], 2 + half)
        parts = []
        for extra in range(ex):
            part = recv_p[half, :, pl.ds(extra * zh * zl, zh * zl), :]
            parts.append(part.reshape(nab, kk))
        high, low = split(jnp.concatenate(parts, axis=1))
        mid[0, 0] = high
        mid[0, 1] = low

        @pl.loop(0, nab // mid_tile)
        def _(step):
            start = pl.multiple_of(step * mid_tile, mid_tile)
            left = (gab[0, 0, pl.ds(start, mid_tile), :], gab[0, 1, pl.ds(start, mid_tile), :])
            value = dot3(left, (mid[0, 0], mid[0, 1])) * sign_mid[half, pl.ds(start, mid_tile), :]
            high, low = split(value)
            mid[1, 0, pl.ds(start, mid_tile), :] = high
            mid[1, 1, pl.ds(start, mid_tile), :] = low

        @pl.loop(0, nab // mid_tile)
        def _(step):
            start = pl.multiple_of(step * mid_tile, mid_tile)
            left = (gab[1, 0, pl.ds(start, mid_tile), :], gab[1, 1, pl.ds(start, mid_tile), :])
            value = dot3(left, (mid[1, 0], mid[1, 1]))
            places = mid_tile // na
            for extra in range(ex):
                part = value[:, extra * kk : (extra + 1) * kk].reshape(places, zh, yc, kk)
                send_b[half, pl.ds(step * places, places), :, pl.ds(extra * yc, yc), :] = part

        send_b_half(half)

    def last_layer(half, group):
        @pl.loop(0, steps)
        def _(step):
            parts = []
            for n in range(together):
                for extra in range(ex):
                    for x in range(xc):
                        row = extra * yc + step * together + n
                        parts.append(recv_b[half, pl.ds(x * zl, zl), group, row, :])
            block = jnp.concatenate(parts, axis=0)
            block = dot3(split(block), (gk[1, 0], gk[1, 1]))
            high, low = split(block)
            rows = mm // halves
            block = dot3((gm_end[half, 0], gm_end[half, 1]), (beside(high, rows), beside(low, rows)))
            for n in range(together):
                a = group * yc + step * together + n
                value = block[:, n * kk : (n + 1) * kk]
                out[a] = value if half == 0 else (out[a] + value) * sign_end[a]

    for half in range(halves):
        middle(half)
    build_k(1)
    build_m_end()
    build_sign_end()
    wait_all(recv_b.at[0], 4)
    for group in range(zh):
        last_layer(0, group)
    for group, sems in b_parts(1):
        wait_all(recv_b.at[1, :, group], sems)
        last_layer(1, group)

    for half in range(halves):
        wait_sent(send_z.at[half, pl.ds(0, nz - 1)], half)
        wait_sent(send_p.at[half, pl.ds(0, np_ - 1)], 2 + half)
    wait_sent(send_b.at[0, pl.ds(0, nb - 1)], 4)
    for group, sems in b_parts(1):
        wait_sent(send_b.at[1, pl.ds(0, nb - 1), group], sems)


def per_device(amplitudes, angles, hadamard, cz_pairs):
    count_a, count_b = lax.axis_size("qa"), lax.axis_size("qb")
    x_total, mm, kk = amplitudes.shape[2:]
    zh, xc = Z_HALVES, X_CHIPS
    yc, zl = count_a // zh, count_b // xc
    halves = 2
    ex = mm // (halves * zl * xc)
    sizes = (zh, zl, xc, yc, halves, ex, kk)
    nab = count_a * count_b
    layers, rotated = angles.shape
    pairs = cz_pairs.shape[1]
    shape_z = (halves, zh * zl, yc, ex * xc, kk)
    shape_p = (halves, xc * yc, ex * zh * zl, kk)
    shape_b = (halves, xc * zl, zh, ex * yc, kk)
    result = pl.pallas_call(
        functools.partial(kernel, sizes),
        out_shape=jax.ShapeDtypeStruct((count_a, mm, kk), F32),
        in_specs=[pl.BlockSpec(memory_space=IN_SPACE)] * 4,
        out_specs=pl.BlockSpec(memory_space=pltpu.VMEM),
        scratch_shapes=[
            pltpu.VMEM(shape_z, F32),
            pltpu.VMEM(shape_z, F32),
            pltpu.VMEM(shape_p, F32),
            pltpu.VMEM(shape_p, F32),
            pltpu.VMEM(shape_b, F32),
            pltpu.VMEM(shape_b, F32),
            pltpu.VMEM((2, 2, kk, kk), BF16),
            pltpu.VMEM((2, mm, mm), BF16),
            pltpu.VMEM((halves, 2, mm, mm // halves), BF16),
            pltpu.VMEM((2, 2, nab, nab), BF16),
            pltpu.VMEM((halves, nab, ex * kk), F32),
            pltpu.VMEM((count_a, mm, kk), F32),
            pltpu.VMEM((2, 2, nab, ex * kk), BF16),
            pltpu.VMEM((x_total, mm, kk), F32),
            pltpu.VMEM((layers, rotated), F32),
            pltpu.VMEM((layers, rotated), jnp.int32),
            pltpu.VMEM((4, layers, rotated), F32),
            pltpu.SMEM((4, layers, rotated), F32),
            pltpu.SMEM((layers, 2, pairs), jnp.int32),
            pltpu.SemaphoreType.DMA((5 + zh,)),
            pltpu.SemaphoreType.DMA((5 + zh,)),
            pltpu.SemaphoreType.DMA((7,)),
        ],
        compiler_params=pltpu.CompilerParams(
            collective_id=0, has_side_effects=True, vmem_limit_bytes=52 * 2**20
        ),
    )(
        amplitudes.reshape(x_total, mm, kk),
        angles,
        hadamard,
        jnp.transpose(cz_pairs, (0, 2, 1)),
    )
    return result.reshape(1, 1, count_a, mm, kk)


def solution(mesh):
    return jax.shard_map(
        per_device,
        mesh=mesh,
        in_specs=(P("qa", "qb", None, None, None), P(), P(), P()),
        out_specs=P("qa", "qb", None, None, None),
        check_vma=False,
    )
```

```python
import functools
import math

import jax
import jax.numpy as jnp
from jax import lax
from jax.experimental import pallas as pl
from jax.experimental.pallas import tpu as pltpu
from jax.sharding import PartitionSpec as P

MESH = pl.DeviceIdType.MESH
F32 = jnp.float32
BF16 = jnp.bfloat16

Z_HALVES = 2
X_CHIPS = 4


def gate_entries(angle, flag):
    cos_part, sin_part = jnp.cos(angle), jnp.sin(angle)
    weight = flag.astype(F32)
    root = math.sqrt(0.5)
    stay, mix, turn = 1.0 - weight + weight * root, weight * root, 1.0 - weight - weight * root
    return (
        cos_part * stay - sin_part * mix,
        cos_part * mix - sin_part * turn,
        sin_part * stay + cos_part * mix,
        sin_part * mix + cos_part * turn,
    )


def split(value):
    high = value.astype(BF16)
    return high, (value - high.astype(F32)).astype(BF16)


def dot3(left, right):
    dot = functools.partial(jnp.dot, preferred_element_type=F32)
    return dot(left[0], right[0]) + (dot(left[0], right[1]) + dot(left[1], right[0]))


def log2(value):
    return value.bit_length() - 1


def kernel(
    sizes,
    amp_in, angles_in, flags_in, pairs_in, out,
    send_z, recv_z, send_p, recv_p, send_b, recv_b,
    gk, gm, gm_end, gab, sign_mid, sign_end, mid,
    amp, angles, flags, entries, gates, pairs, send_sem, recv_sem, load_sem,
):
    zh, zl, xc, yc, halves, ex, kk = sizes
    nz, np_, nb, na = zh * zl, xc * yc, xc * zl, zh * yc
    mm = halves * zl * ex * xc
    nab = na * nb
    bits_a, bits_b, bits_x, bits_m, bits_k = log2(na), log2(nb), log2(na), log2(mm), log2(kk)
    qubits = bits_a + bits_b + bits_x + bits_m + bits_k
    shift_m = bits_k
    shift_x = shift_m + bits_m
    shift_b = shift_x + bits_x
    shift_a = shift_b + bits_b
    rot_m = bits_a + bits_b
    rot_k = rot_m + bits_m
    sub = ex * xc
    together = 4
    steps = yc // together if yc > together else 1
    together = yc // steps

    me_a, me_b = lax.axis_index("qa"), lax.axis_index("qb")
    my_zh, my_yc = lax.div(me_a, yc), lax.rem(me_a, yc)
    my_x, my_zl = lax.div(me_b, zl), lax.rem(me_b, zl)
    my_z = my_zh * zl + my_zl
    my_p = my_x * yc + my_yc

    def at_z(other, step):
        z_half = lax.rem(my_zh + other, zh)
        z_low = lax.rem(my_zl + step, zl)
        return z_half * zl + z_low, (z_half * yc + my_yc, my_x * zl + z_low)

    def at_p(step):
        p = lax.rem(my_p + step, np_)
        return p, (my_zh * yc + lax.rem(p, yc), lax.div(p, yc) * zl + my_zl)

    run = zl // 2

    def at_b(other, step):
        side = lax.rem(lax.div(my_zl, run) + other, 2)
        place = side * run + lax.rem(my_zl + step, run)
        b = lax.rem(my_x + lax.div(step, run), xc) * zl + place
        return b, (me_a, b)

    barrier = pltpu.get_barrier_semaphore()

    def signal(device):
        pl.semaphore_signal(barrier, inc=1, device_id=device, device_id_type=MESH)

    for other in (1, 0):
        pl.loop(1 - other, zl)(lambda step, other=other: signal(at_z(other, step)[1]))
    for other in (1, 0):
        pl.loop(1 - other, nb // 2)(lambda step, other=other: signal(at_b(other, step)[1]))
    pl.loop(1, np_)(lambda step: signal(at_p(step)[1]))

    def load(number, source, target):
        return pltpu.make_async_copy(source, target, load_sem.at[number])

    small = [load(0, angles_in, angles), load(1, flags_in, flags), load(2, pairs_in, pairs)]
    for copy in small:
        copy.start()

    def amp_part(number):
        z_half = lax.rem(my_zh + 1 + number // steps, zh)
        first = z_half * yc + number % steps * together
        part = pl.ds(first, together)
        return z_half, first, load(3 + number, amp_in.at[part], amp.at[part])

    for number in range(zh * steps):
        amp_part(number)[2].start()

    small[0].wait()
    small[1].wait()
    for number, value in enumerate(gate_entries(angles[...], flags[...])):
        entries[number] = value
    to_scalars = load(0, entries, gates)
    to_scalars.start()
    small[2].wait()
    to_scalars.wait()

    def entry(layer, qubit, out_one, in_one):
        value = lambda number: gates[number, layer, qubit]
        return jnp.where(
            out_one,
            jnp.where(in_one, value(3), value(2)),
            jnp.where(in_one, value(1), value(0)),
        )

    def matrix(layer, out_index, in_index, qubits_and_bits):
        result = None
        for qubit, out_bit, in_bit in qubits_and_bits:
            factor = entry(
                layer, qubit, (out_index & (1 << out_bit)) != 0, (in_index & (1 << in_bit)) != 0
            )
            result = factor if result is None else result * factor
        return result

    def signs(layer, index):
        odd = jnp.zeros(index.shape, jnp.int32)
        for pair in range(pairs.shape[2]):
            mask = jnp.left_shift(1, qubits - 1 - pairs[layer, 0, pair]) | jnp.left_shift(
                1, qubits - 1 - pairs[layer, 1, pair]
            )
            odd = odd ^ jnp.where((index & mask) == mask, 1, 0)
        return 1.0 - 2.0 * odd.astype(F32)

    def build_k(layer):
        rows = lax.broadcasted_iota(jnp.int32, (kk, kk), 0)
        cols = lax.broadcasted_iota(jnp.int32, (kk, kk), 1)
        bits = [(rot_k + n, bits_k - 1 - n, bits_k - 1 - n) for n in range(bits_k)]
        gk[layer, 0], gk[layer, 1] = split(matrix(layer, cols, rows, bits))

    bits_zl, bits_xc, bits_ex, bits_h = log2(zl), log2(xc), log2(ex), log2(halves)

    natural = [bits_m - 1 - n for n in range(bits_m)]

    def build_m():
        rows = lax.broadcasted_iota(jnp.int32, (mm, mm), 0)
        cols = lax.broadcasted_iota(jnp.int32, (mm, mm), 1)
        bits = [(rot_m + n, natural[n], natural[n]) for n in range(bits_m)]
        gm[0], gm[1] = split(matrix(0, rows, cols, bits))

    def build_m_end():
        columns = mm // halves
        rows = lax.broadcasted_iota(jnp.int32, (mm, columns), 0)
        in_bits = (
            natural[:bits_h]
            + [bits_zl - 1 - n for n in range(bits_zl)]
            + [bits_zl + bits_xc + bits_ex - 1 - n for n in range(bits_ex)]
            + [bits_zl + bits_xc - 1 - n for n in range(bits_xc)]
        )
        bits = [(rot_m + n, natural[n], in_bits[n]) for n in range(bits_m)]
        for half in range(halves):
            cols = lax.broadcasted_iota(jnp.int32, (mm, columns), 1) + half * columns
            gm_end[half, 0], gm_end[half, 1] = split(matrix(1, rows, cols, bits))

    bits_yc, bits_zh = log2(yc), log2(zh)

    def mid_bits():
        a_bits = [bits_zl + bits_zh - 1 - n for n in range(bits_zh)]
        a_bits += [bits_zl + bits_zh + bits_yc - 1 - n for n in range(bits_yc)]
        b_bits = [bits_zl + bits_zh + bits_yc + bits_xc - 1 - n for n in range(bits_xc)]
        b_bits += [bits_zl - 1 - n for n in range(bits_zl)]
        return a_bits + b_bits

    tile = min(nab, 64)

    def build_ab(layer):
        mids = mid_bits()
        if layer == 0:
            outs = mids
        else:
            outs = [bits_a - 1 - n for n in range(bits_a)]
            outs += [bits_a + bits_b - 1 - n for n in range(bits_b)]
        bits = [(n, outs[n], mids[n]) for n in range(bits_a + bits_b)]

        @pl.loop(0, nab // tile)
        def _(step):
            start = pl.multiple_of(step * tile, tile)
            rows = lax.broadcasted_iota(jnp.int32, (tile, nab), 0) + start
            cols = lax.broadcasted_iota(jnp.int32, (tile, nab), 1)
            high, low = split(matrix(layer, rows, cols, bits))
            gab[layer, 0, pl.ds(start, tile), :] = high
            gab[layer, 1, pl.ds(start, tile), :] = low

    sign_tile = min(nab, 128)

    def build_sign_mid():
        mids = mid_bits()
        per = nab // sign_tile

        @pl.loop(0, halves * ex * per)
        def _(step):
            part, start = lax.div(step, per), pl.multiple_of(lax.rem(step, per) * sign_tile, sign_tile)
            half, extra = lax.div(part, ex), lax.rem(part, ex)
            rows = lax.broadcasted_iota(jnp.int32, (sign_tile, kk), 0) + start
            cols = lax.broadcasted_iota(jnp.int32, (sign_tile, kk), 1)
            index = cols
            for n in range(bits_a + bits_b):
                index = index | (((rows >> mids[n]) & 1) << (qubits - 1 - n))
            m = ((half * zl + my_zl) * ex + extra) * xc + my_x
            index = index + (m * (1 << shift_m) + me_a * (1 << shift_x))
            sign_mid[half, pl.ds(start, sign_tile), pl.ds(pl.multiple_of(extra * kk, kk), kk)] = signs(0, index)

    def build_sign_end():
        @pl.loop(0, na)
        def _(a):
            rows = lax.broadcasted_iota(jnp.int32, (mm, kk), 0)
            cols = lax.broadcasted_iota(jnp.int32, (mm, kk), 1)
            index = cols + rows * (1 << shift_m)
            index = index + (me_a * (1 << shift_x) + me_b * (1 << shift_b) + a * (1 << shift_a))
            sign_end[a] = signs(1, index)

    def beside(value, rows):
        parts = [value[n * rows : (n + 1) * rows] for n in range(together)]
        return jnp.concatenate(parts, axis=1)

    def layer_0(number):
        z_half, first, copy = amp_part(number)
        copy.wait()
        block = amp[pl.ds(first, together)].reshape(together * mm, kk)
        block = dot3(split(block), (gk[0, 0], gk[0, 1]))
        high, low = split(block)
        block = dot3((gm[0], gm[1]), (beside(high, mm), beside(low, mm)))
        for n in range(together):
            done = block[:, n * kk : (n + 1) * kk].reshape(halves, zl, sub, kk)
            send_z[:, pl.ds(z_half * zl, zl), number % steps * together + n] = done

    def send(source, target, sems, device):
        pltpu.make_async_remote_copy(
            src_ref=source,
            dst_ref=target,
            send_sem=send_sem.at[sems],
            recv_sem=recv_sem.at[sems],
            device_id=device,
            device_id_type=MESH,
        ).start()

    def keep(source, target, sems):
        pltpu.make_async_copy(source, target, recv_sem.at[sems]).start()

    def wait_all(target, sems):
        pltpu.make_async_copy(target, target, recv_sem.at[sems]).wait()

    def wait_sent(part, sems):
        pltpu.make_async_copy(part, part, send_sem.at[sems]).wait()

    def send_z_part(half, other):
        @pl.loop(1 - other, zl)
        def _(step):
            number, device = at_z(other, step)
            send(send_z.at[half, number], recv_z.at[half, my_z], half, device)

    def keep_z(half):
        keep(send_z.at[half, my_z], recv_z.at[half, my_z], half)

    def send_p_half(half):
        @pl.loop(1, np_)
        def _(step):
            number, device = at_p(step)
            send(send_p.at[half, number], recv_p.at[half, my_p], 2 + half, device)

        keep(send_p.at[half, my_p], recv_p.at[half, my_p], 2 + half)

    def b_part(ref, half, number, group):
        return ref.at[half, number] if half == 0 else ref.at[half, number, group]

    def b_parts(half):
        return [(0, 4)] if half == 0 else [(group, 5 + group) for group in range(zh)]

    def send_b_half(half):
        for group, sems in b_parts(half):
            for other in (1, 0):
                @pl.loop(1 - other, nb // 2)
                def _(step):
                    number, device = at_b(other, step)
                    send(b_part(send_b, half, number, group), b_part(recv_b, half, me_b, group), sems, device)

            keep(b_part(send_b, half, me_b, group), b_part(recv_b, half, me_b, group), sems)

    build_k(0)
    build_m()
    for number in range(steps):
        layer_0(number)
    pl.semaphore_wait(barrier, nz + np_ + nb - 3)
    send_z_part(0, 1)
    for number in range(steps, zh * steps):
        layer_0(number)
    send_z_part(0, 0)
    keep_z(0)
    send_z_part(1, 1)
    send_z_part(1, 0)
    keep_z(1)

    build_ab(0)
    build_ab(1)
    build_sign_mid()
    mid_tile = min(nab, 128)

    def middle(half):
        wait_all(recv_z.at[half], half)

        @pl.loop(0, yc)
        def _(xr):
            for z_half in range(zh):
                for low in range(sub):
                    rows = recv_z[half, pl.ds(z_half * zl, zl), xr, low, :]
                    extra, x = low // xc, low % xc
                    send_p[half, x * yc + xr, pl.ds((extra * zh + z_half) * zl, zl), :] = rows

        send_p_half(half)
        wait_all(recv_p.at[half], 2 + half)
        parts = []
        for extra in range(ex):
            part = recv_p[half, :, pl.ds(extra * zh * zl, zh * zl), :]
            parts.append(part.reshape(nab, kk))
        high, low = split(jnp.concatenate(parts, axis=1))
        mid[0, 0] = high
        mid[0, 1] = low

        @pl.loop(0, nab // mid_tile)
        def _(step):
            start = pl.multiple_of(step * mid_tile, mid_tile)
            left = (gab[0, 0, pl.ds(start, mid_tile), :], gab[0, 1, pl.ds(start, mid_tile), :])
            value = dot3(left, (mid[0, 0], mid[0, 1])) * sign_mid[half, pl.ds(start, mid_tile), :]
            high, low = split(value)
            mid[1, 0, pl.ds(start, mid_tile), :] = high
            mid[1, 1, pl.ds(start, mid_tile), :] = low

        @pl.loop(0, nab // mid_tile)
        def _(step):
            start = pl.multiple_of(step * mid_tile, mid_tile)
            left = (gab[1, 0, pl.ds(start, mid_tile), :], gab[1, 1, pl.ds(start, mid_tile), :])
            value = dot3(left, (mid[1, 0], mid[1, 1]))
            places = mid_tile // na
            for extra in range(ex):
                part = value[:, extra * kk : (extra + 1) * kk].reshape(places, zh, yc, kk)
                send_b[half, pl.ds(step * places, places), :, pl.ds(extra * yc, yc), :] = part

        send_b_half(half)

    def last_layer(half, group):
        @pl.loop(0, steps)
        def _(step):
            parts = []
            for n in range(together):
                for extra in range(ex):
                    for x in range(xc):
                        row = extra * yc + step * together + n
                        parts.append(recv_b[half, pl.ds(x * zl, zl), group, row, :])
            block = jnp.concatenate(parts, axis=0)
            block = dot3(split(block), (gk[1, 0], gk[1, 1]))
            high, low = split(block)
            rows = mm // halves
            block = dot3((gm_end[half, 0], gm_end[half, 1]), (beside(high, rows), beside(low, rows)))
            for n in range(together):
                a = group * yc + step * together + n
                value = block[:, n * kk : (n + 1) * kk]
                out[a] = value if half == 0 else (out[a] + value) * sign_end[a]

    for half in range(halves):
        middle(half)
    build_k(1)
    build_m_end()
    build_sign_end()
    wait_all(recv_b.at[0], 4)
    for group in range(zh):
        last_layer(0, group)
    for group, sems in b_parts(1):
        wait_all(recv_b.at[1, :, group], sems)
        last_layer(1, group)

    for half in range(halves):
        wait_sent(send_z.at[half, pl.ds(0, nz - 1)], half)
        wait_sent(send_p.at[half, pl.ds(0, np_ - 1)], 2 + half)
    wait_sent(send_b.at[0, pl.ds(0, nb - 1)], 4)
    for group, sems in b_parts(1):
        wait_sent(send_b.at[1, pl.ds(0, nb - 1), group], sems)


def per_device(amplitudes, angles, hadamard, cz_pairs):
    count_a, count_b = lax.axis_size("qa"), lax.axis_size("qb")
    x_total, mm, kk = amplitudes.shape[2:]
    zh, xc = Z_HALVES, X_CHIPS
    yc, zl = count_a // zh, count_b // xc
    halves = 2
    ex = mm // (halves * zl * xc)
    sizes = (zh, zl, xc, yc, halves, ex, kk)
    nab = count_a * count_b
    layers, rotated = angles.shape
    pairs = cz_pairs.shape[1]
    shape_z = (halves, zh * zl, yc, ex * xc, kk)
    shape_p = (halves, xc * yc, ex * zh * zl, kk)
    shape_b = (halves, xc * zl, zh, ex * yc, kk)
    result = pl.pallas_call(
        functools.partial(kernel, sizes),
        out_shape=jax.ShapeDtypeStruct((count_a, mm, kk), F32),
        in_specs=[pl.BlockSpec(memory_space=pltpu.HBM)] * 4,
        out_specs=pl.BlockSpec(memory_space=pltpu.VMEM),
        scratch_shapes=[
            pltpu.VMEM(shape_z, F32),
            pltpu.VMEM(shape_z, F32),
            pltpu.VMEM(shape_p, F32),
            pltpu.VMEM(shape_p, F32),
            pltpu.VMEM(shape_b, F32),
            pltpu.VMEM(shape_b, F32),
            pltpu.VMEM((2, 2, kk, kk), BF16),
            pltpu.VMEM((2, mm, mm), BF16),
            pltpu.VMEM((halves, 2, mm, mm // halves), BF16),
            pltpu.VMEM((2, 2, nab, nab), BF16),
            pltpu.VMEM((halves, nab, ex * kk), F32),
            pltpu.VMEM((count_a, mm, kk), F32),
            pltpu.VMEM((2, 2, nab, ex * kk), BF16),
            pltpu.VMEM((x_total, mm, kk), F32),
            pltpu.VMEM((layers, rotated), F32),
            pltpu.VMEM((layers, rotated), jnp.int32),
            pltpu.VMEM((4, layers, rotated), F32),
            pltpu.SMEM((4, layers, rotated), F32),
            pltpu.SMEM((layers, 2, pairs), jnp.int32),
            pltpu.SemaphoreType.DMA((5 + zh,)),
            pltpu.SemaphoreType.DMA((5 + zh,)),
            pltpu.SemaphoreType.DMA((7,)),
        ],
        compiler_params=pltpu.CompilerParams(
            collective_id=0, has_side_effects=True, vmem_limit_bytes=40 * 2**20
        ),
    )(*(
        pltpu.with_memory_space_constraint(value, pltpu.HBM)
        for value in (
            amplitudes.reshape(x_total, mm, kk),
            angles,
            hadamard,
            jnp.transpose(cz_pairs, (0, 2, 1)),
        )
    ))
    return result.reshape(1, 1, count_a, mm, kk)


def solution(mesh):
    return jax.shard_map(
        per_device,
        mesh=mesh,
        in_specs=(P("qa", "qb", None, None, None), P(), P(), P()),
        out_specs=P("qa", "qb", None, None, None),
        check_vma=False,
    )
```

```python
import functools
import math

import jax
import jax.numpy as jnp
from jax import lax
from jax.experimental import pallas as pl
from jax.experimental.pallas import tpu as pltpu
from jax.sharding import PartitionSpec as P

MESH = pl.DeviceIdType.MESH
F32 = jnp.float32
BF16 = jnp.bfloat16

Z_HALVES = 2
X_CHIPS = 4


def gate_entries(angle, flag):
    cos_part, sin_part = jnp.cos(angle), jnp.sin(angle)
    weight = flag.astype(F32)
    root = math.sqrt(0.5)
    stay, mix, turn = 1.0 - weight + weight * root, weight * root, 1.0 - weight - weight * root
    return (
        cos_part * stay - sin_part * mix,
        cos_part * mix - sin_part * turn,
        sin_part * stay + cos_part * mix,
        sin_part * mix + cos_part * turn,
    )


def split(value):
    high = value.astype(BF16)
    return high, (value - high.astype(F32)).astype(BF16)


def dot3(left, right):
    dot = functools.partial(jnp.dot, preferred_element_type=F32)
    return dot(left[0], right[0]) + (dot(left[0], right[1]) + dot(left[1], right[0]))


def log2(value):
    return value.bit_length() - 1


def kernel(
    sizes,
    amp_in, angles_in, flags_in, pairs_in, out,
    send_z, recv_z, send_p, recv_p, send_b, recv_b,
    gk, gm, gm_end, gab, sign_mid, sign_end, mid,
    amp, angles, flags, entries, gates, pairs, send_sem, recv_sem, load_sem,
):
    zh, zl, xc, yc, halves, ex, kk = sizes
    nz, np_, nb, na = zh * zl, xc * yc, xc * zl, zh * yc
    mm = halves * zl * ex * xc
    nab = na * nb
    bits_a, bits_b, bits_x, bits_m, bits_k = log2(na), log2(nb), log2(na), log2(mm), log2(kk)
    qubits = bits_a + bits_b + bits_x + bits_m + bits_k
    shift_m = bits_k
    shift_x = shift_m + bits_m
    shift_b = shift_x + bits_x
    shift_a = shift_b + bits_b
    rot_m = bits_a + bits_b
    rot_k = rot_m + bits_m
    sub = ex * xc
    together = 4
    steps = yc // together if yc > together else 1
    together = yc // steps

    me_a, me_b = lax.axis_index("qa"), lax.axis_index("qb")
    my_zh, my_yc = lax.div(me_a, yc), lax.rem(me_a, yc)
    my_x, my_zl = lax.div(me_b, zl), lax.rem(me_b, zl)
    my_z = my_zh * zl + my_zl
    my_p = my_x * yc + my_yc

    def at_z(other, step):
        z_half = lax.rem(my_zh + other, zh)
        z_low = lax.rem(my_zl + step, zl)
        return z_half * zl + z_low, (z_half * yc + my_yc, my_x * zl + z_low)

    def at_p(step):
        p = lax.rem(my_p + step, np_)
        return p, (my_zh * yc + lax.rem(p, yc), lax.div(p, yc) * zl + my_zl)

    run = zl // 2

    def at_b(other, step):
        side = lax.rem(lax.div(my_zl, run) + other, 2)
        place = side * run + lax.rem(my_zl + step, run)
        b = lax.rem(my_x + lax.div(step, run), xc) * zl + place
        return b, (me_a, b)

    barrier = pltpu.get_barrier_semaphore()

    def signal(device):
        pl.semaphore_signal(barrier, inc=1, device_id=device, device_id_type=MESH)

    for other in (1, 0):
        pl.loop(1 - other, zl)(lambda step, other=other: signal(at_z(other, step)[1]))
    pl.loop(1, np_)(lambda step: signal(at_p(step)[1]))

    def load(number, source, target):
        return pltpu.make_async_copy(source, target, load_sem.at[number])

    small = [load(0, angles_in, angles), load(1, flags_in, flags), load(2, pairs_in, pairs)]
    for copy in small:
        copy.start()

    def amp_part(number):
        z_half = lax.rem(my_zh + 1 + number // steps, zh)
        first = z_half * yc + number % steps * together
        part = pl.ds(first, together)
        return z_half, first, load(3 + number, amp_in.at[part], amp.at[part])

    for number in range(zh * steps):
        amp_part(number)[2].start()

    small[0].wait()
    small[1].wait()
    for number, value in enumerate(gate_entries(angles[...], flags[...])):
        entries[number] = value
    to_scalars = load(0, entries, gates)
    to_scalars.start()
    small[2].wait()
    to_scalars.wait()

    def entry(layer, qubit, out_one, in_one):
        value = lambda number: gates[number, layer, qubit]
        return jnp.where(
            out_one,
            jnp.where(in_one, value(3), value(2)),
            jnp.where(in_one, value(1), value(0)),
        )

    def matrix(layer, out_index, in_index, qubits_and_bits):
        result = None
        for qubit, out_bit, in_bit in qubits_and_bits:
            factor = entry(
                layer, qubit, (out_index & (1 << out_bit)) != 0, (in_index & (1 << in_bit)) != 0
            )
            result = factor if result is None else result * factor
        return result

    def signs(layer, index):
        odd = jnp.zeros(index.shape, jnp.int32)
        for pair in range(pairs.shape[2]):
            mask = jnp.left_shift(1, qubits - 1 - pairs[layer, 0, pair]) | jnp.left_shift(
                1, qubits - 1 - pairs[layer, 1, pair]
            )
            odd = odd ^ jnp.where((index & mask) == mask, 1, 0)
        return 1.0 - 2.0 * odd.astype(F32)

    def build_k(layer):
        rows = lax.broadcasted_iota(jnp.int32, (kk, kk), 0)
        cols = lax.broadcasted_iota(jnp.int32, (kk, kk), 1)
        bits = [(rot_k + n, bits_k - 1 - n, bits_k - 1 - n) for n in range(bits_k)]
        gk[layer, 0], gk[layer, 1] = split(matrix(layer, cols, rows, bits))

    bits_zl, bits_xc, bits_ex, bits_h = log2(zl), log2(xc), log2(ex), log2(halves)

    natural = [bits_m - 1 - n for n in range(bits_m)]

    def build_m():
        rows = lax.broadcasted_iota(jnp.int32, (mm, mm), 0)
        cols = lax.broadcasted_iota(jnp.int32, (mm, mm), 1)
        bits = [(rot_m + n, natural[n], natural[n]) for n in range(bits_m)]
        gm[0], gm[1] = split(matrix(0, rows, cols, bits))

    def build_m_end():
        columns = mm // halves
        rows = lax.broadcasted_iota(jnp.int32, (mm, columns), 0)
        in_bits = (
            natural[:bits_h]
            + [bits_zl - 1 - n for n in range(bits_zl)]
            + [bits_zl + bits_xc + bits_ex - 1 - n for n in range(bits_ex)]
            + [bits_zl + bits_xc - 1 - n for n in range(bits_xc)]
        )
        bits = [(rot_m + n, natural[n], in_bits[n]) for n in range(bits_m)]
        for half in range(halves):
            cols = lax.broadcasted_iota(jnp.int32, (mm, columns), 1) + half * columns
            gm_end[half, 0], gm_end[half, 1] = split(matrix(1, rows, cols, bits))

    bits_yc, bits_zh = log2(yc), log2(zh)

    def mid_bits():
        a_bits = [bits_zl + bits_zh - 1 - n for n in range(bits_zh)]
        a_bits += [bits_zl + bits_zh + bits_yc - 1 - n for n in range(bits_yc)]
        b_bits = [bits_zl + bits_zh + bits_yc + bits_xc - 1 - n for n in range(bits_xc)]
        b_bits += [bits_zl - 1 - n for n in range(bits_zl)]
        return a_bits + b_bits

    tile = min(nab, 64)

    def build_ab(layer):
        mids = mid_bits()
        if layer == 0:
            outs = mids
        else:
            outs = [bits_a - 1 - n for n in range(bits_a)]
            outs += [bits_a + bits_b - 1 - n for n in range(bits_b)]
        bits = [(n, outs[n], mids[n]) for n in range(bits_a + bits_b)]

        @pl.loop(0, nab // tile)
        def _(step):
            start = pl.multiple_of(step * tile, tile)
            rows = lax.broadcasted_iota(jnp.int32, (tile, nab), 0) + start
            cols = lax.broadcasted_iota(jnp.int32, (tile, nab), 1)
            high, low = split(matrix(layer, rows, cols, bits))
            gab[layer, 0, pl.ds(start, tile), :] = high
            gab[layer, 1, pl.ds(start, tile), :] = low

    sign_tile = min(nab, 128)

    def build_sign_mid():
        mids = mid_bits()
        per = nab // sign_tile

        @pl.loop(0, halves * ex * per)
        def _(step):
            part, start = lax.div(step, per), pl.multiple_of(lax.rem(step, per) * sign_tile, sign_tile)
            half, extra = lax.div(part, ex), lax.rem(part, ex)
            rows = lax.broadcasted_iota(jnp.int32, (sign_tile, kk), 0) + start
            cols = lax.broadcasted_iota(jnp.int32, (sign_tile, kk), 1)
            index = cols
            for n in range(bits_a + bits_b):
                index = index | (((rows >> mids[n]) & 1) << (qubits - 1 - n))
            m = ((half * zl + my_zl) * ex + extra) * xc + my_x
            index = index + (m * (1 << shift_m) + me_a * (1 << shift_x))
            sign_mid[half, pl.ds(start, sign_tile), pl.ds(pl.multiple_of(extra * kk, kk), kk)] = signs(0, index)

    def build_sign_end():
        @pl.loop(0, na)
        def _(a):
            rows = lax.broadcasted_iota(jnp.int32, (mm, kk), 0)
            cols = lax.broadcasted_iota(jnp.int32, (mm, kk), 1)
            index = cols + rows * (1 << shift_m)
            index = index + (me_a * (1 << shift_x) + me_b * (1 << shift_b) + a * (1 << shift_a))
            sign_end[a] = signs(1, index)

    def beside(value, rows):
        parts = [value[n * rows : (n + 1) * rows] for n in range(together)]
        return jnp.concatenate(parts, axis=1)

    def layer_0(number):
        z_half, first, copy = amp_part(number)
        copy.wait()
        block = amp[pl.ds(first, together)].reshape(together * mm, kk)
        block = dot3(split(block), (gk[0, 0], gk[0, 1]))
        high, low = split(block)
        block = dot3((gm[0], gm[1]), (beside(high, mm), beside(low, mm)))
        for n in range(together):
            done = block[:, n * kk : (n + 1) * kk].reshape(halves, zl, sub, kk)
            send_z[:, pl.ds(z_half * zl, zl), number % steps * together + n] = done

    def send(source, target, sems, device):
        pltpu.make_async_remote_copy(
            src_ref=source,
            dst_ref=target,
            send_sem=send_sem.at[sems],
            recv_sem=recv_sem.at[sems],
            device_id=device,
            device_id_type=MESH,
        ).start()

    def keep(source, target, sems):
        pltpu.make_async_copy(source, target, recv_sem.at[sems]).start()

    def wait_all(target, sems):
        pltpu.make_async_copy(target, target, recv_sem.at[sems]).wait()

    def wait_sent(part, sems):
        pltpu.make_async_copy(part, part, send_sem.at[sems]).wait()

    def send_z_part(half, other):
        @pl.loop(1 - other, zl)
        def _(step):
            number, device = at_z(other, step)
            send(send_z.at[half, number], recv_z.at[half, my_z], half, device)

    def keep_z(half):
        keep(send_z.at[half, my_z], recv_z.at[half, my_z], half)

    def send_p_half(half):
        @pl.loop(1, np_)
        def _(step):
            number, device = at_p(step)
            send(send_p.at[half, number], recv_p.at[half, my_p], 2 + half, device)

        keep(send_p.at[half, my_p], recv_p.at[half, my_p], 2 + half)

    def b_part(ref, half, number, group):
        return ref.at[half, number] if half == 0 else ref.at[half, number, group]

    def b_parts(half):
        return [(0, 4)] if half == 0 else [(group, 5 + group) for group in range(zh)]

    def send_b_half(half):
        for group, sems in b_parts(half):
            for other in (1, 0):
                @pl.loop(1 - other, nb // 2)
                def _(step):
                    number, device = at_b(other, step)
                    send(b_part(send_b, half, number, group), b_part(recv_b, half, me_b, group), sems, device)

            keep(b_part(send_b, half, me_b, group), b_part(recv_b, half, me_b, group), sems)

    build_k(0)
    build_m()
    for number in range(steps):
        layer_0(number)
    pl.semaphore_wait(barrier, nz + np_ - 2)
    send_z_part(0, 1)
    for number in range(steps, zh * steps):
        layer_0(number)
    send_z_part(0, 0)
    keep_z(0)
    send_z_part(1, 1)
    send_z_part(1, 0)
    keep_z(1)

    build_ab(0)
    build_ab(1)
    build_sign_mid()
    mid_tile = min(nab, 128)

    def middle(half):
        wait_all(recv_z.at[half], half)

        @pl.loop(0, yc)
        def _(xr):
            for z_half in range(zh):
                for low in range(sub):
                    rows = recv_z[half, pl.ds(z_half * zl, zl), xr, low, :]
                    extra, x = low // xc, low % xc
                    send_p[half, x * yc + xr, pl.ds((extra * zh + z_half) * zl, zl), :] = rows

        send_p_half(half)
        wait_all(recv_p.at[half], 2 + half)
        parts = []
        for extra in range(ex):
            part = recv_p[half, :, pl.ds(extra * zh * zl, zh * zl), :]
            parts.append(part.reshape(nab, kk))
        high, low = split(jnp.concatenate(parts, axis=1))
        mid[0, 0] = high
        mid[0, 1] = low

        @pl.loop(0, nab // mid_tile)
        def _(step):
            start = pl.multiple_of(step * mid_tile, mid_tile)
            left = (gab[0, 0, pl.ds(start, mid_tile), :], gab[0, 1, pl.ds(start, mid_tile), :])
            value = dot3(left, (mid[0, 0], mid[0, 1])) * sign_mid[half, pl.ds(start, mid_tile), :]
            high, low = split(value)
            mid[1, 0, pl.ds(start, mid_tile), :] = high
            mid[1, 1, pl.ds(start, mid_tile), :] = low

        @pl.loop(0, nab // mid_tile)
        def _(step):
            start = pl.multiple_of(step * mid_tile, mid_tile)
            left = (gab[1, 0, pl.ds(start, mid_tile), :], gab[1, 1, pl.ds(start, mid_tile), :])
            value = dot3(left, (mid[1, 0], mid[1, 1]))
            places = mid_tile // na
            for extra in range(ex):
                part = value[:, extra * kk : (extra + 1) * kk].reshape(places, zh, yc, kk)
                send_b[half, pl.ds(step * places, places), :, pl.ds(extra * yc, yc), :] = part

        send_b_half(half)

    def last_layer(half, group):
        @pl.loop(0, steps)
        def _(step):
            parts = []
            for n in range(together):
                for extra in range(ex):
                    for x in range(xc):
                        row = extra * yc + step * together + n
                        parts.append(recv_b[half, pl.ds(x * zl, zl), group, row, :])
            block = jnp.concatenate(parts, axis=0)
            block = dot3(split(block), (gk[1, 0], gk[1, 1]))
            high, low = split(block)
            rows = mm // halves
            block = dot3((gm_end[half, 0], gm_end[half, 1]), (beside(high, rows), beside(low, rows)))
            for n in range(together):
                a = group * yc + step * together + n
                value = block[:, n * kk : (n + 1) * kk]
                out[a] = value if half == 0 else (out[a] + value) * sign_end[a]

    for half in range(halves):
        middle(half)
    build_k(1)
    build_m_end()
    build_sign_end()
    wait_all(recv_b.at[0], 4)
    for group in range(zh):
        last_layer(0, group)
    for group, sems in b_parts(1):
        wait_all(recv_b.at[1, :, group], sems)
        last_layer(1, group)

    for half in range(halves):
        wait_sent(send_z.at[half, pl.ds(0, nz - 1)], half)
        wait_sent(send_p.at[half, pl.ds(0, np_ - 1)], 2 + half)
    wait_sent(send_b.at[0, pl.ds(0, nb - 1)], 4)
    for group, sems in b_parts(1):
        wait_sent(send_b.at[1, pl.ds(0, nb - 1), group], sems)


def per_device(amplitudes, angles, hadamard, cz_pairs):
    count_a, count_b = lax.axis_size("qa"), lax.axis_size("qb")
    x_total, mm, kk = amplitudes.shape[2:]
    zh, xc = Z_HALVES, X_CHIPS
    yc, zl = count_a // zh, count_b // xc
    halves = 2
    ex = mm // (halves * zl * xc)
    sizes = (zh, zl, xc, yc, halves, ex, kk)
    nab = count_a * count_b
    layers, rotated = angles.shape
    pairs = cz_pairs.shape[1]
    shape_z = (halves, zh * zl, yc, ex * xc, kk)
    shape_p = (halves, xc * yc, ex * zh * zl, kk)
    shape_b = (halves, xc * zl, zh, ex * yc, kk)
    result = pl.pallas_call(
        functools.partial(kernel, sizes),
        out_shape=jax.ShapeDtypeStruct((count_a, mm, kk), F32),
        in_specs=[pl.BlockSpec(memory_space=pltpu.HBM)] * 4,
        out_specs=pl.BlockSpec(memory_space=pltpu.VMEM),
        scratch_shapes=[
            pltpu.VMEM(shape_z, F32),
            pltpu.VMEM(shape_z, F32),
            pltpu.VMEM(shape_p, F32),
            pltpu.VMEM(shape_p, F32),
            pltpu.VMEM(shape_b, F32),
            pltpu.VMEM(shape_b, F32),
            pltpu.VMEM((2, 2, kk, kk), BF16),
            pltpu.VMEM((2, mm, mm), BF16),
            pltpu.VMEM((halves, 2, mm, mm // halves), BF16),
            pltpu.VMEM((2, 2, nab, nab), BF16),
            pltpu.VMEM((halves, nab, ex * kk), F32),
            pltpu.VMEM((count_a, mm, kk), F32),
            pltpu.VMEM((2, 2, nab, ex * kk), BF16),
            pltpu.VMEM((x_total, mm, kk), F32),
            pltpu.VMEM((layers, rotated), F32),
            pltpu.VMEM((layers, rotated), jnp.int32),
            pltpu.VMEM((4, layers, rotated), F32),
            pltpu.SMEM((4, layers, rotated), F32),
            pltpu.SMEM((layers, 2, pairs), jnp.int32),
            pltpu.SemaphoreType.DMA((5 + zh,)),
            pltpu.SemaphoreType.DMA((5 + zh,)),
            pltpu.SemaphoreType.DMA((7,)),
        ],
        compiler_params=pltpu.CompilerParams(
            collective_id=0, has_side_effects=True, vmem_limit_bytes=40 * 2**20
        ),
    )(*(
        pltpu.with_memory_space_constraint(value, pltpu.HBM)
        for value in (
            amplitudes.reshape(x_total, mm, kk),
            angles,
            hadamard,
            jnp.transpose(cz_pairs, (0, 2, 1)),
        )
    ))
    return result.reshape(1, 1, count_a, mm, kk)


def solution(mesh):
    return jax.shard_map(
        per_device,
        mesh=mesh,
        in_specs=(P("qa", "qb", None, None, None), P(), P(), P()),
        out_specs=P("qa", "qb", None, None, None),
        check_vma=False,
    )
```

```python
import functools
import math

import jax
import jax.numpy as jnp
from jax import lax
from jax.experimental import pallas as pl
from jax.experimental.pallas import tpu as pltpu
from jax.sharding import PartitionSpec as P

MESH = pl.DeviceIdType.MESH
F32 = jnp.float32
BF16 = jnp.bfloat16

Z_HALVES = 2
X_CHIPS = 4


def gate_entries(angle, flag):
    cos_part, sin_part = jnp.cos(angle), jnp.sin(angle)
    weight = flag.astype(F32)
    root = math.sqrt(0.5)
    stay, mix, turn = 1.0 - weight + weight * root, weight * root, 1.0 - weight - weight * root
    return (
        cos_part * stay - sin_part * mix,
        cos_part * mix - sin_part * turn,
        sin_part * stay + cos_part * mix,
        sin_part * mix + cos_part * turn,
    )


def split(value):
    high = value.astype(BF16)
    return high, (value - high.astype(F32)).astype(BF16)


def dot3(left, right):
    dot = functools.partial(jnp.dot, preferred_element_type=F32)
    return dot(left[0], right[0]) + (dot(left[0], right[1]) + dot(left[1], right[0]))


def log2(value):
    return value.bit_length() - 1


def kernel(
    sizes,
    amp_in, angles_in, flags_in, pairs_in, out,
    send_z, recv_z, send_p, recv_p, send_b, recv_b,
    gk, gm, gm_end, gab, sign_mid, sign_end, mid,
    amp, angles, flags, entries, gates, pairs, send_sem, recv_sem, load_sem, go_z, runs_sem, go_p,
):
    zh, zl, xc, yc, halves, ex, kk = sizes
    nz, np_, nb, na = zh * zl, xc * yc, xc * zl, zh * yc
    mm = halves * zl * ex * xc
    nab = na * nb
    bits_a, bits_b, bits_x, bits_m, bits_k = log2(na), log2(nb), log2(na), log2(mm), log2(kk)
    qubits = bits_a + bits_b + bits_x + bits_m + bits_k
    shift_m = bits_k
    shift_x = shift_m + bits_m
    shift_b = shift_x + bits_x
    shift_a = shift_b + bits_b
    rot_m = bits_a + bits_b
    rot_k = rot_m + bits_m
    sub = ex * xc
    together = 4
    steps = yc // together if yc > together else 1
    together = yc // steps

    me_a, me_b = lax.axis_index("qa"), lax.axis_index("qb")
    my_zh, my_yc = lax.div(me_a, yc), lax.rem(me_a, yc)
    my_x, my_zl = lax.div(me_b, zl), lax.rem(me_b, zl)
    my_z = my_zh * zl + my_zl
    my_p = my_x * yc + my_yc

    def at_z(other, step):
        z_half = lax.rem(my_zh + other, zh)
        z_low = lax.rem(my_zl + step, zl)
        return z_half * zl + z_low, (z_half * yc + my_yc, my_x * zl + z_low)

    def at_p(step):
        p = lax.rem(my_p + step, np_)
        return p, (my_zh * yc + lax.rem(p, yc), lax.div(p, yc) * zl + my_zl)

    run = zl // 2

    def at_b(other, step):
        side = lax.rem(lax.div(my_zl, run) + other, 2)
        place = side * run + lax.rem(my_zl + step, run)
        b = lax.rem(my_x + lax.div(step, run), xc) * zl + place
        return b, (me_a, b)

    barrier = pltpu.get_barrier_semaphore()

    def signal(device, semaphore=barrier):
        pl.semaphore_signal(semaphore, inc=1, device_id=device, device_id_type=MESH)

    def to_p(semaphore):
        pl.loop(1, np_)(lambda step: signal(at_p(step)[1], semaphore))

    def to_other_run(semaphore):
        pl.loop(0, zl)(lambda step: signal(at_z(1, step)[1], semaphore))

    second = my_zh == 1
    pl.loop(1, zl)(lambda step: signal(at_z(0, step)[1]))
    pl.when(jnp.logical_not(second))(lambda: to_other_run(barrier))
    pl.when(second)(lambda: to_p(barrier))

    def load(number, source, target):
        return pltpu.make_async_copy(source, target, load_sem.at[number])

    small = [load(0, angles_in, angles), load(1, flags_in, flags), load(2, pairs_in, pairs)]
    for copy in small:
        copy.start()

    def amp_part(number):
        z_half = number // steps
        first = z_half * yc + number % steps * together
        part = pl.ds(first, together)
        return z_half, first, load(3 + number, amp_in.at[part], amp.at[part])

    for number in range(zh * steps):
        amp_part(number)[2].start()

    small[0].wait()
    small[1].wait()
    for number, value in enumerate(gate_entries(angles[...], flags[...])):
        entries[number] = value
    to_scalars = load(0, entries, gates)
    to_scalars.start()
    small[2].wait()
    to_scalars.wait()

    def entry(layer, qubit, out_one, in_one):
        value = lambda number: gates[number, layer, qubit]
        return jnp.where(
            out_one,
            jnp.where(in_one, value(3), value(2)),
            jnp.where(in_one, value(1), value(0)),
        )

    def matrix(layer, out_index, in_index, qubits_and_bits):
        result = None
        for qubit, out_bit, in_bit in qubits_and_bits:
            factor = entry(
                layer, qubit, (out_index & (1 << out_bit)) != 0, (in_index & (1 << in_bit)) != 0
            )
            result = factor if result is None else result * factor
        return result

    def signs(layer, index):
        odd = jnp.zeros(index.shape, jnp.int32)
        for pair in range(pairs.shape[2]):
            mask = jnp.left_shift(1, qubits - 1 - pairs[layer, 0, pair]) | jnp.left_shift(
                1, qubits - 1 - pairs[layer, 1, pair]
            )
            odd = odd ^ jnp.where((index & mask) == mask, 1, 0)
        return 1.0 - 2.0 * odd.astype(F32)

    def build_k(layer):
        rows = lax.broadcasted_iota(jnp.int32, (kk, kk), 0)
        cols = lax.broadcasted_iota(jnp.int32, (kk, kk), 1)
        bits = [(rot_k + n, bits_k - 1 - n, bits_k - 1 - n) for n in range(bits_k)]
        gk[layer, 0], gk[layer, 1] = split(matrix(layer, cols, rows, bits))

    bits_zl, bits_xc, bits_ex, bits_h = log2(zl), log2(xc), log2(ex), log2(halves)

    natural = [bits_m - 1 - n for n in range(bits_m)]

    def build_m():
        rows = lax.broadcasted_iota(jnp.int32, (mm, mm), 0)
        cols = lax.broadcasted_iota(jnp.int32, (mm, mm), 1)
        bits = [(rot_m + n, natural[n], natural[n]) for n in range(bits_m)]
        gm[0], gm[1] = split(matrix(0, rows, cols, bits))

    def build_m_end():
        columns = mm // halves
        rows = lax.broadcasted_iota(jnp.int32, (mm, columns), 0)
        in_bits = (
            natural[:bits_h]
            + [bits_zl - 1 - n for n in range(bits_zl)]
            + [bits_zl + bits_xc + bits_ex - 1 - n for n in range(bits_ex)]
            + [bits_zl + bits_xc - 1 - n for n in range(bits_xc)]
        )
        bits = [(rot_m + n, natural[n], in_bits[n]) for n in range(bits_m)]
        for half in range(halves):
            cols = lax.broadcasted_iota(jnp.int32, (mm, columns), 1) + half * columns
            gm_end[half, 0], gm_end[half, 1] = split(matrix(1, rows, cols, bits))

    bits_yc, bits_zh = log2(yc), log2(zh)

    def mid_bits():
        a_bits = [bits_zl + bits_zh - 1 - n for n in range(bits_zh)]
        a_bits += [bits_zl + bits_zh + bits_yc - 1 - n for n in range(bits_yc)]
        b_bits = [bits_zl + bits_zh + bits_yc + bits_xc - 1 - n for n in range(bits_xc)]
        b_bits += [bits_zl - 1 - n for n in range(bits_zl)]
        return a_bits + b_bits

    tile = min(nab, 64)

    def build_ab(layer):
        mids = mid_bits()
        if layer == 0:
            outs = mids
        else:
            outs = [bits_a - 1 - n for n in range(bits_a)]
            outs += [bits_a + bits_b - 1 - n for n in range(bits_b)]
        bits = [(n, outs[n], mids[n]) for n in range(bits_a + bits_b)]

        @pl.loop(0, nab // tile)
        def _(step):
            start = pl.multiple_of(step * tile, tile)
            rows = lax.broadcasted_iota(jnp.int32, (tile, nab), 0) + start
            cols = lax.broadcasted_iota(jnp.int32, (tile, nab), 1)
            high, low = split(matrix(layer, rows, cols, bits))
            gab[layer, 0, pl.ds(start, tile), :] = high
            gab[layer, 1, pl.ds(start, tile), :] = low

    sign_tile = min(nab, 128)

    def build_sign_mid():
        mids = mid_bits()
        per = nab // sign_tile

        @pl.loop(0, halves * ex * per)
        def _(step):
            part, start = lax.div(step, per), pl.multiple_of(lax.rem(step, per) * sign_tile, sign_tile)
            half, extra = lax.div(part, ex), lax.rem(part, ex)
            rows = lax.broadcasted_iota(jnp.int32, (sign_tile, kk), 0) + start
            cols = lax.broadcasted_iota(jnp.int32, (sign_tile, kk), 1)
            index = cols
            for n in range(bits_a + bits_b):
                index = index | (((rows >> mids[n]) & 1) << (qubits - 1 - n))
            m = ((half * zl + my_zl) * ex + extra) * xc + my_x
            index = index + (m * (1 << shift_m) + me_a * (1 << shift_x))
            sign_mid[half, pl.ds(start, sign_tile), pl.ds(pl.multiple_of(extra * kk, kk), kk)] = signs(0, index)

    def build_sign_end():
        @pl.loop(0, na)
        def _(a):
            rows = lax.broadcasted_iota(jnp.int32, (mm, kk), 0)
            cols = lax.broadcasted_iota(jnp.int32, (mm, kk), 1)
            index = cols + rows * (1 << shift_m)
            index = index + (me_a * (1 << shift_x) + me_b * (1 << shift_b) + a * (1 << shift_a))
            sign_end[a] = signs(1, index)

    def beside(value, rows):
        parts = [value[n * rows : (n + 1) * rows] for n in range(together)]
        return jnp.concatenate(parts, axis=1)

    def layer_0(number):
        z_half, first, copy = amp_part(number)
        copy.wait()
        block = amp[pl.ds(first, together)].reshape(together * mm, kk)
        block = dot3(split(block), (gk[0, 0], gk[0, 1]))
        high, low = split(block)
        block = dot3((gm[0], gm[1]), (beside(high, mm), beside(low, mm)))
        for n in range(together):
            done = block[:, n * kk : (n + 1) * kk].reshape(halves, zl, sub, kk)
            send_z[:, pl.ds(z_half * zl, zl), number % steps * together + n] = done

    def send(source, target, sems, device):
        pltpu.make_async_remote_copy(
            src_ref=source,
            dst_ref=target,
            send_sem=send_sem.at[sems],
            recv_sem=recv_sem.at[sems],
            device_id=device,
            device_id_type=MESH,
        ).start()

    def keep(source, target, sems):
        pltpu.make_async_copy(source, target, recv_sem.at[sems]).start()

    def wait_all(target, sems):
        pltpu.make_async_copy(target, target, recv_sem.at[sems]).wait()

    def wait_sent(part, sems):
        pltpu.make_async_copy(part, part, send_sem.at[sems]).wait()

    def send_z_part(half, other):
        @pl.loop(1 - other, zl)
        def _(step):
            number, device = at_z(other, step)
            send(send_z.at[half, number], recv_z.at[half, my_z], half, device)

    def keep_z(half):
        keep(send_z.at[half, my_z], recv_z.at[half, my_z], half)

    def send_p_half(half):
        @pl.loop(1, np_)
        def _(step):
            number, device = at_p(step)
            send(send_p.at[half, number], recv_p.at[half, my_p], 2 + half, device)

        keep(send_p.at[half, my_p], recv_p.at[half, my_p], 2 + half)

    def b_part(ref, half, number, group):
        return ref.at[half, number] if half == 0 else ref.at[half, number, group]

    def b_parts(half):
        return [(0, 4)] if half == 0 else [(group, 5 + group) for group in range(zh)]

    def send_b_half(half):
        for group, sems in b_parts(half):
            for other in (1, 0):
                @pl.loop(1 - other, nb // 2)
                def _(step):
                    number, device = at_b(other, step)
                    send(b_part(send_b, half, number, group), b_part(recv_b, half, me_b, group), sems, device)

            keep(b_part(send_b, half, me_b, group), b_part(recv_b, half, me_b, group), sems)

    build_k(0)
    build_m()
    for number in range(steps):
        layer_0(number)
    pl.semaphore_wait(barrier, zl - 1 + my_zh * (zl + np_ - 1))
    pl.when(second)(lambda: to_other_run(go_z))
    send_z_part(0, my_zh)
    pl.when(second)(lambda: to_p(runs_sem))
    for number in range(steps, zh * steps):
        layer_0(number)

    @pl.when(jnp.logical_not(second))
    def _():
        pl.semaphore_wait(go_z, zl)

    send_z_part(0, 1 - my_zh)
    keep_z(0)
    send_z_part(1, my_zh)
    send_z_part(1, 1 - my_zh)
    keep_z(1)

    @pl.when(second)
    def _():
        pl.semaphore_wait(runs_sem, np_ - 1)
        signal(at_z(1, 0)[1], go_p)

    build_ab(0)
    build_ab(1)
    build_sign_mid()
    mid_tile = min(nab, 128)

    def middle(half):
        wait_all(recv_z.at[half], half)

        @pl.loop(0, yc)
        def _(xr):
            for z_half in range(zh):
                for low in range(sub):
                    rows = recv_z[half, pl.ds(z_half * zl, zl), xr, low, :]
                    extra, x = low // xc, low % xc
                    send_p[half, x * yc + xr, pl.ds((extra * zh + z_half) * zl, zl), :] = rows

        if half == 0:
            @pl.when(jnp.logical_not(second))
            def _():
                pl.semaphore_wait(go_p, 1)

        send_p_half(half)
        wait_all(recv_p.at[half], 2 + half)
        parts = []
        for extra in range(ex):
            part = recv_p[half, :, pl.ds(extra * zh * zl, zh * zl), :]
            parts.append(part.reshape(nab, kk))
        high, low = split(jnp.concatenate(parts, axis=1))
        mid[0, 0] = high
        mid[0, 1] = low

        @pl.loop(0, nab // mid_tile)
        def _(step):
            start = pl.multiple_of(step * mid_tile, mid_tile)
            left = (gab[0, 0, pl.ds(start, mid_tile), :], gab[0, 1, pl.ds(start, mid_tile), :])
            value = dot3(left, (mid[0, 0], mid[0, 1])) * sign_mid[half, pl.ds(start, mid_tile), :]
            high, low = split(value)
            mid[1, 0, pl.ds(start, mid_tile), :] = high
            mid[1, 1, pl.ds(start, mid_tile), :] = low

        @pl.loop(0, nab // mid_tile)
        def _(step):
            start = pl.multiple_of(step * mid_tile, mid_tile)
            left = (gab[1, 0, pl.ds(start, mid_tile), :], gab[1, 1, pl.ds(start, mid_tile), :])
            value = dot3(left, (mid[1, 0], mid[1, 1]))
            places = mid_tile // na
            for extra in range(ex):
                part = value[:, extra * kk : (extra + 1) * kk].reshape(places, zh, yc, kk)
                send_b[half, pl.ds(step * places, places), :, pl.ds(extra * yc, yc), :] = part

        send_b_half(half)

    def last_layer(half, group):
        @pl.loop(0, steps)
        def _(step):
            parts = []
            for n in range(together):
                for extra in range(ex):
                    for x in range(xc):
                        row = extra * yc + step * together + n
                        parts.append(recv_b[half, pl.ds(x * zl, zl), group, row, :])
            block = jnp.concatenate(parts, axis=0)
            block = dot3(split(block), (gk[1, 0], gk[1, 1]))
            high, low = split(block)
            rows = mm // halves
            block = dot3((gm_end[half, 0], gm_end[half, 1]), (beside(high, rows), beside(low, rows)))
            for n in range(together):
                a = group * yc + step * together + n
                value = block[:, n * kk : (n + 1) * kk]
                out[a] = value if half == 0 else (out[a] + value) * sign_end[a]

    for half in range(halves):
        middle(half)
    build_k(1)
    build_m_end()
    build_sign_end()
    wait_all(recv_b.at[0], 4)
    for group in range(zh):
        last_layer(0, group)
    for group, sems in b_parts(1):
        wait_all(recv_b.at[1, :, group], sems)
        last_layer(1, group)

    for half in range(halves):
        wait_sent(send_z.at[half, pl.ds(0, nz - 1)], half)
        wait_sent(send_p.at[half, pl.ds(0, np_ - 1)], 2 + half)
    wait_sent(send_b.at[0, pl.ds(0, nb - 1)], 4)
    for group, sems in b_parts(1):
        wait_sent(send_b.at[1, pl.ds(0, nb - 1), group], sems)


def per_device(amplitudes, angles, hadamard, cz_pairs):
    count_a, count_b = lax.axis_size("qa"), lax.axis_size("qb")
    x_total, mm, kk = amplitudes.shape[2:]
    zh, xc = Z_HALVES, X_CHIPS
    yc, zl = count_a // zh, count_b // xc
    halves = 2
    ex = mm // (halves * zl * xc)
    sizes = (zh, zl, xc, yc, halves, ex, kk)
    nab = count_a * count_b
    layers, rotated = angles.shape
    pairs = cz_pairs.shape[1]
    shape_z = (halves, zh * zl, yc, ex * xc, kk)
    shape_p = (halves, xc * yc, ex * zh * zl, kk)
    shape_b = (halves, xc * zl, zh, ex * yc, kk)
    result = pl.pallas_call(
        functools.partial(kernel, sizes),
        out_shape=jax.ShapeDtypeStruct((count_a, mm, kk), F32),
        in_specs=[pl.BlockSpec(memory_space=pltpu.HBM)] * 4,
        out_specs=pl.BlockSpec(memory_space=pltpu.VMEM),
        scratch_shapes=[
            pltpu.VMEM(shape_z, F32),
            pltpu.VMEM(shape_z, F32),
            pltpu.VMEM(shape_p, F32),
            pltpu.VMEM(shape_p, F32),
            pltpu.VMEM(shape_b, F32),
            pltpu.VMEM(shape_b, F32),
            pltpu.VMEM((2, 2, kk, kk), BF16),
            pltpu.VMEM((2, mm, mm), BF16),
            pltpu.VMEM((halves, 2, mm, mm // halves), BF16),
            pltpu.VMEM((2, 2, nab, nab), BF16),
            pltpu.VMEM((halves, nab, ex * kk), F32),
            pltpu.VMEM((count_a, mm, kk), F32),
            pltpu.VMEM((2, 2, nab, ex * kk), BF16),
            pltpu.VMEM((x_total, mm, kk), F32),
            pltpu.VMEM((layers, rotated), F32),
            pltpu.VMEM((layers, rotated), jnp.int32),
            pltpu.VMEM((4, layers, rotated), F32),
            pltpu.SMEM((4, layers, rotated), F32),
            pltpu.SMEM((layers, 2, pairs), jnp.int32),
            pltpu.SemaphoreType.DMA((5 + zh,)),
            pltpu.SemaphoreType.DMA((5 + zh,)),
            pltpu.SemaphoreType.DMA((7,)),
            pltpu.SemaphoreType.REGULAR,
            pltpu.SemaphoreType.REGULAR,
            pltpu.SemaphoreType.REGULAR,
        ],
        compiler_params=pltpu.CompilerParams(
            collective_id=0, has_side_effects=True, vmem_limit_bytes=40 * 2**20
        ),
    )(*(
        pltpu.with_memory_space_constraint(value, pltpu.HBM)
        for value in (
            amplitudes.reshape(x_total, mm, kk),
            angles,
            hadamard,
            jnp.transpose(cz_pairs, (0, 2, 1)),
        )
    ))
    return result.reshape(1, 1, count_a, mm, kk)


def solution(mesh):
    return jax.shard_map(
        per_device,
        mesh=mesh,
        in_specs=(P("qa", "qb", None, None, None), P(), P(), P()),
        out_specs=P("qa", "qb", None, None, None),
        check_vma=False,
    )
```

```python
import functools
import math

import jax
import jax.numpy as jnp
from jax import lax
from jax.experimental import pallas as pl
from jax.experimental.pallas import tpu as pltpu
from jax.sharding import PartitionSpec as P

MESH = pl.DeviceIdType.MESH
F32 = jnp.float32
BF16 = jnp.bfloat16

Z_HALVES = 2
X_CHIPS = 4


def gate_entries(angle, flag):
    cos_part, sin_part = jnp.cos(angle), jnp.sin(angle)
    weight = flag.astype(F32)
    root = math.sqrt(0.5)
    stay, mix, turn = 1.0 - weight + weight * root, weight * root, 1.0 - weight - weight * root
    return (
        cos_part * stay - sin_part * mix,
        cos_part * mix - sin_part * turn,
        sin_part * stay + cos_part * mix,
        sin_part * mix + cos_part * turn,
    )


def split(value):
    high = value.astype(BF16)
    return high, (value - high.astype(F32)).astype(BF16)


def dot3(left, right):
    dot = functools.partial(jnp.dot, preferred_element_type=F32)
    return dot(left[0], right[0]) + (dot(left[0], right[1]) + dot(left[1], right[0]))


def log2(value):
    return value.bit_length() - 1


def kernel(
    sizes,
    amp_in, angles_in, flags_in, pairs_in, out,
    send_z, recv_z, send_p, recv_p, send_b, recv_b,
    gk, gm, gm_end, gab, sign_mid, sign_end, mid,
    amp, angles, flags, entries, gates, pairs, send_sem, recv_sem, load_sem, go_z, runs_sem, go_p,
):
    zh, zl, xc, yc, halves, ex, kk = sizes
    nz, np_, nb, na = zh * zl, xc * yc, xc * zl, zh * yc
    mm = halves * zl * ex * xc
    nab = na * nb
    bits_a, bits_b, bits_x, bits_m, bits_k = log2(na), log2(nb), log2(na), log2(mm), log2(kk)
    qubits = bits_a + bits_b + bits_x + bits_m + bits_k
    shift_m = bits_k
    shift_x = shift_m + bits_m
    shift_b = shift_x + bits_x
    shift_a = shift_b + bits_b
    rot_m = bits_a + bits_b
    rot_k = rot_m + bits_m
    sub = ex * xc
    together = 4
    steps = yc // together if yc > together else 1
    together = yc // steps

    me_a, me_b = lax.axis_index("qa"), lax.axis_index("qb")
    my_zh, my_yc = lax.div(me_a, yc), lax.rem(me_a, yc)
    my_x, my_zl = lax.div(me_b, zl), lax.rem(me_b, zl)
    my_z = my_zh * zl + my_zl
    my_p = my_x * yc + my_yc

    def at_z(other, step):
        z_half = lax.rem(my_zh + other, zh)
        z_low = lax.rem(my_zl + step, zl)
        return z_half * zl + z_low, (z_half * yc + my_yc, my_x * zl + z_low)

    def at_p(step):
        p = lax.rem(my_p + step, np_)
        return p, (my_zh * yc + lax.rem(p, yc), lax.div(p, yc) * zl + my_zl)

    run = zl // 2

    def at_b(other, step):
        side = lax.rem(lax.div(my_zl, run) + other, 2)
        place = side * run + lax.rem(my_zl + step, run)
        b = lax.rem(my_x + lax.div(step, run), xc) * zl + place
        return b, (me_a, b)

    barrier = pltpu.get_barrier_semaphore()

    def signal(device, semaphore=barrier):
        pl.semaphore_signal(semaphore, inc=1, device_id=device, device_id_type=MESH)

    def to_p(semaphore):
        pl.loop(1, np_)(lambda step: signal(at_p(step)[1], semaphore))

    def to_other_run(semaphore):
        pl.loop(0, zl)(lambda step: signal(at_z(1, step)[1], semaphore))

    second = my_zh == 1
    pl.loop(1, zl)(lambda step: signal(at_z(0, step)[1]))
    pl.when(jnp.logical_not(second))(lambda: to_other_run(barrier))
    pl.when(second)(lambda: to_p(barrier))

    def load(number, source, target):
        return pltpu.make_async_copy(source, target, load_sem.at[number])

    small = [load(0, angles_in, angles), load(1, flags_in, flags), load(2, pairs_in, pairs)]
    for copy in small:
        copy.start()

    def amp_part(number):
        z_half = number // steps
        first = z_half * yc + number % steps * together
        part = pl.ds(first, together)
        return z_half, first, load(3 + number, amp_in.at[part], amp.at[part])

    for number in range(zh * steps):
        amp_part(number)[2].start()

    small[0].wait()
    small[1].wait()
    for number, value in enumerate(gate_entries(angles[...], flags[...])):
        entries[number] = value
    to_scalars = load(0, entries, gates)
    to_scalars.start()
    small[2].wait()
    to_scalars.wait()

    def entry(layer, qubit, out_one, in_one):
        value = lambda number: gates[number, layer, qubit]
        return jnp.where(
            out_one,
            jnp.where(in_one, value(3), value(2)),
            jnp.where(in_one, value(1), value(0)),
        )

    def matrix(layer, out_index, in_index, qubits_and_bits):
        result = None
        for qubit, out_bit, in_bit in qubits_and_bits:
            factor = entry(
                layer, qubit, (out_index & (1 << out_bit)) != 0, (in_index & (1 << in_bit)) != 0
            )
            result = factor if result is None else result * factor
        return result

    def signs(layer, index):
        odd = jnp.zeros(index.shape, jnp.int32)
        for pair in range(pairs.shape[2]):
            mask = jnp.left_shift(1, qubits - 1 - pairs[layer, 0, pair]) | jnp.left_shift(
                1, qubits - 1 - pairs[layer, 1, pair]
            )
            odd = odd ^ jnp.where((index & mask) == mask, 1, 0)
        return 1.0 - 2.0 * odd.astype(F32)

    def build_k(layer):
        rows = lax.broadcasted_iota(jnp.int32, (kk, kk), 0)
        cols = lax.broadcasted_iota(jnp.int32, (kk, kk), 1)
        bits = [(rot_k + n, bits_k - 1 - n, bits_k - 1 - n) for n in range(bits_k)]
        gk[layer, 0], gk[layer, 1] = split(matrix(layer, cols, rows, bits))

    bits_zl, bits_xc, bits_ex, bits_h = log2(zl), log2(xc), log2(ex), log2(halves)

    natural = [bits_m - 1 - n for n in range(bits_m)]

    def build_m():
        rows = lax.broadcasted_iota(jnp.int32, (mm, mm), 0)
        cols = lax.broadcasted_iota(jnp.int32, (mm, mm), 1)
        bits = [(rot_m + n, natural[n], natural[n]) for n in range(bits_m)]
        gm[0], gm[1] = split(matrix(0, rows, cols, bits))

    def build_m_end():
        columns = mm // halves
        rows = lax.broadcasted_iota(jnp.int32, (mm, columns), 0)
        in_bits = (
            natural[:bits_h]
            + [bits_zl - 1 - n for n in range(bits_zl)]
            + [bits_zl + bits_xc + bits_ex - 1 - n for n in range(bits_ex)]
            + [bits_zl + bits_xc - 1 - n for n in range(bits_xc)]
        )
        bits = [(rot_m + n, natural[n], in_bits[n]) for n in range(bits_m)]
        for half in range(halves):
            cols = lax.broadcasted_iota(jnp.int32, (mm, columns), 1) + half * columns
            gm_end[half, 0], gm_end[half, 1] = split(matrix(1, rows, cols, bits))

    bits_yc, bits_zh = log2(yc), log2(zh)

    def mid_bits():
        a_bits = [bits_zl + bits_zh - 1 - n for n in range(bits_zh)]
        a_bits += [bits_zl + bits_zh + bits_yc - 1 - n for n in range(bits_yc)]
        b_bits = [bits_zl + bits_zh + bits_yc + bits_xc - 1 - n for n in range(bits_xc)]
        b_bits += [bits_zl - 1 - n for n in range(bits_zl)]
        return a_bits + b_bits

    tile = min(nab, 64)

    def build_ab(layer):
        mids = mid_bits()
        if layer == 0:
            outs = mids
        else:
            outs = [bits_a - 1 - n for n in range(bits_a)]
            outs += [bits_a + bits_b - 1 - n for n in range(bits_b)]
        bits = [(n, outs[n], mids[n]) for n in range(bits_a + bits_b)]

        @pl.loop(0, nab // tile)
        def _(step):
            start = pl.multiple_of(step * tile, tile)
            rows = lax.broadcasted_iota(jnp.int32, (tile, nab), 0) + start
            cols = lax.broadcasted_iota(jnp.int32, (tile, nab), 1)
            high, low = split(matrix(layer, rows, cols, bits))
            gab[layer, 0, pl.ds(start, tile), :] = high
            gab[layer, 1, pl.ds(start, tile), :] = low

    sign_tile = min(nab, 128)

    def build_sign_mid():
        mids = mid_bits()
        per = nab // sign_tile

        @pl.loop(0, halves * ex * per)
        def _(step):
            part, start = lax.div(step, per), pl.multiple_of(lax.rem(step, per) * sign_tile, sign_tile)
            half, extra = lax.div(part, ex), lax.rem(part, ex)
            rows = lax.broadcasted_iota(jnp.int32, (sign_tile, kk), 0) + start
            cols = lax.broadcasted_iota(jnp.int32, (sign_tile, kk), 1)
            index = cols
            for n in range(bits_a + bits_b):
                index = index | (((rows >> mids[n]) & 1) << (qubits - 1 - n))
            m = ((half * zl + my_zl) * ex + extra) * xc + my_x
            index = index + (m * (1 << shift_m) + me_a * (1 << shift_x))
            sign_mid[half, pl.ds(start, sign_tile), pl.ds(pl.multiple_of(extra * kk, kk), kk)] = signs(0, index)

    def build_sign_end():
        @pl.loop(0, na)
        def _(a):
            rows = lax.broadcasted_iota(jnp.int32, (mm, kk), 0)
            cols = lax.broadcasted_iota(jnp.int32, (mm, kk), 1)
            index = cols + rows * (1 << shift_m)
            index = index + (me_a * (1 << shift_x) + me_b * (1 << shift_b) + a * (1 << shift_a))
            sign_end[a] = signs(1, index)

    def beside(value, rows):
        parts = [value[n * rows : (n + 1) * rows] for n in range(together)]
        return jnp.concatenate(parts, axis=1)

    def layer_0(number):
        z_half, first, copy = amp_part(number)
        copy.wait()
        block = amp[pl.ds(first, together)].reshape(together * mm, kk)
        block = dot3(split(block), (gk[0, 0], gk[0, 1]))
        high, low = split(block)
        block = dot3((gm[0], gm[1]), (beside(high, mm), beside(low, mm)))
        for n in range(together):
            done = block[:, n * kk : (n + 1) * kk].reshape(halves, zl, sub, kk)
            send_z[:, pl.ds(z_half * zl, zl), number % steps * together + n] = done

    def send(source, target, sems, device):
        pltpu.make_async_remote_copy(
            src_ref=source,
            dst_ref=target,
            send_sem=send_sem.at[sems],
            recv_sem=recv_sem.at[sems],
            device_id=device,
            device_id_type=MESH,
        ).start()

    def keep(source, target, sems):
        pltpu.make_async_copy(source, target, recv_sem.at[sems]).start()

    def wait_all(target, sems):
        pltpu.make_async_copy(target, target, recv_sem.at[sems]).wait()

    def wait_sent(part, sems):
        pltpu.make_async_copy(part, part, send_sem.at[sems]).wait()

    def send_z_part(half, other):
        @pl.loop(1 - other, zl)
        def _(step):
            number, device = at_z(other, step)
            send(send_z.at[half, number], recv_z.at[half, my_z], half, device)

    def keep_z(half):
        keep(send_z.at[half, my_z], recv_z.at[half, my_z], half)

    def send_p_half(half):
        @pl.loop(1, np_)
        def _(step):
            number, device = at_p(step)
            send(send_p.at[half, number], recv_p.at[half, my_p], 2 + half, device)

        keep(send_p.at[half, my_p], recv_p.at[half, my_p], 2 + half)

    def b_part(ref, half, number, group):
        return ref.at[half, number] if half == 0 else ref.at[half, number, group]

    def b_parts(half):
        return [(0, 4)] if half == 0 else [(group, 5 + group) for group in range(zh)]

    def send_b_half(half):
        for group, sems in b_parts(half):
            @pl.loop(1, nb)
            def _(step):
                number = lax.rem(me_b + step, nb)
                send(b_part(send_b, half, number, group), b_part(recv_b, half, me_b, group), sems, (me_a, number))

            keep(b_part(send_b, half, me_b, group), b_part(recv_b, half, me_b, group), sems)

    build_k(0)
    build_m()
    for number in range(steps):
        layer_0(number)
    pl.semaphore_wait(barrier, zl - 1 + my_zh * (zl + np_ - 1))
    pl.when(second)(lambda: to_other_run(go_z))
    send_z_part(0, my_zh)
    pl.when(second)(lambda: to_p(runs_sem))
    for number in range(steps, zh * steps):
        layer_0(number)

    @pl.when(jnp.logical_not(second))
    def _():
        build_ab(0)
        pl.semaphore_wait(go_z, zl)

    send_z_part(0, 1 - my_zh)
    keep_z(0)
    send_z_part(1, my_zh)
    send_z_part(1, 1 - my_zh)
    keep_z(1)

    @pl.when(second)
    def _():
        pl.semaphore_wait(runs_sem, np_ - 1)
        signal(at_z(1, 0)[1], go_p)

    pl.when(second)(lambda: build_ab(0))
    build_ab(1)
    build_sign_mid()
    mid_tile = min(nab, 128)

    def middle(half):
        wait_all(recv_z.at[half], half)

        @pl.loop(0, yc)
        def _(xr):
            for z_half in range(zh):
                for low in range(sub):
                    rows = recv_z[half, pl.ds(z_half * zl, zl), xr, low, :]
                    extra, x = low // xc, low % xc
                    send_p[half, x * yc + xr, pl.ds((extra * zh + z_half) * zl, zl), :] = rows

        if half == 0:
            @pl.when(jnp.logical_not(second))
            def _():
                pl.semaphore_wait(go_p, 1)

        send_p_half(half)
        wait_all(recv_p.at[half], 2 + half)
        parts = []
        for extra in range(ex):
            part = recv_p[half, :, pl.ds(extra * zh * zl, zh * zl), :]
            parts.append(part.reshape(nab, kk))
        high, low = split(jnp.concatenate(parts, axis=1))
        mid[0, 0] = high
        mid[0, 1] = low

        @pl.loop(0, nab // mid_tile)
        def _(step):
            start = pl.multiple_of(step * mid_tile, mid_tile)
            left = (gab[0, 0, pl.ds(start, mid_tile), :], gab[0, 1, pl.ds(start, mid_tile), :])
            value = dot3(left, (mid[0, 0], mid[0, 1])) * sign_mid[half, pl.ds(start, mid_tile), :]
            high, low = split(value)
            mid[1, 0, pl.ds(start, mid_tile), :] = high
            mid[1, 1, pl.ds(start, mid_tile), :] = low

        @pl.loop(0, nab // mid_tile)
        def _(step):
            start = pl.multiple_of(step * mid_tile, mid_tile)
            left = (gab[1, 0, pl.ds(start, mid_tile), :], gab[1, 1, pl.ds(start, mid_tile), :])
            value = dot3(left, (mid[1, 0], mid[1, 1]))
            places = mid_tile // na
            for extra in range(ex):
                part = value[:, extra * kk : (extra + 1) * kk].reshape(places, zh, yc, kk)
                send_b[half, pl.ds(step * places, places), :, pl.ds(extra * yc, yc), :] = part

        send_b_half(half)

    def last_layer(half, group):
        @pl.loop(0, steps)
        def _(step):
            parts = []
            for n in range(together):
                for extra in range(ex):
                    for x in range(xc):
                        row = extra * yc + step * together + n
                        parts.append(recv_b[half, pl.ds(x * zl, zl), group, row, :])
            block = jnp.concatenate(parts, axis=0)
            block = dot3(split(block), (gk[1, 0], gk[1, 1]))
            high, low = split(block)
            rows = mm // halves
            block = dot3((gm_end[half, 0], gm_end[half, 1]), (beside(high, rows), beside(low, rows)))
            for n in range(together):
                a = group * yc + step * together + n
                value = block[:, n * kk : (n + 1) * kk]
                out[a] = value if half == 0 else (out[a] + value) * sign_end[a]

    for half in range(halves):
        middle(half)
    build_k(1)
    build_m_end()
    build_sign_end()
    wait_all(recv_b.at[0], 4)
    for group in range(zh):
        last_layer(0, group)
    for group, sems in b_parts(1):
        wait_all(recv_b.at[1, :, group], sems)
        last_layer(1, group)

    for half in range(halves):
        wait_sent(send_z.at[half, pl.ds(0, nz - 1)], half)
        wait_sent(send_p.at[half, pl.ds(0, np_ - 1)], 2 + half)
    wait_sent(send_b.at[0, pl.ds(0, nb - 1)], 4)
    for group, sems in b_parts(1):
        wait_sent(send_b.at[1, pl.ds(0, nb - 1), group], sems)


def per_device(amplitudes, angles, hadamard, cz_pairs):
    count_a, count_b = lax.axis_size("qa"), lax.axis_size("qb")
    x_total, mm, kk = amplitudes.shape[2:]
    zh, xc = Z_HALVES, X_CHIPS
    yc, zl = count_a // zh, count_b // xc
    halves = 2
    ex = mm // (halves * zl * xc)
    sizes = (zh, zl, xc, yc, halves, ex, kk)
    nab = count_a * count_b
    layers, rotated = angles.shape
    pairs = cz_pairs.shape[1]
    shape_z = (halves, zh * zl, yc, ex * xc, kk)
    shape_p = (halves, xc * yc, ex * zh * zl, kk)
    shape_b = (halves, xc * zl, zh, ex * yc, kk)
    result = pl.pallas_call(
        functools.partial(kernel, sizes),
        out_shape=jax.ShapeDtypeStruct((count_a, mm, kk), F32),
        in_specs=[pl.BlockSpec(memory_space=pltpu.HBM)] * 4,
        out_specs=pl.BlockSpec(memory_space=pltpu.VMEM),
        scratch_shapes=[
            pltpu.VMEM(shape_z, F32),
            pltpu.VMEM(shape_z, F32),
            pltpu.VMEM(shape_p, F32),
            pltpu.VMEM(shape_p, F32),
            pltpu.VMEM(shape_b, F32),
            pltpu.VMEM(shape_b, F32),
            pltpu.VMEM((2, 2, kk, kk), BF16),
            pltpu.VMEM((2, mm, mm), BF16),
            pltpu.VMEM((halves, 2, mm, mm // halves), BF16),
            pltpu.VMEM((2, 2, nab, nab), BF16),
            pltpu.VMEM((halves, nab, ex * kk), F32),
            pltpu.VMEM((count_a, mm, kk), F32),
            pltpu.VMEM((2, 2, nab, ex * kk), BF16),
            pltpu.VMEM((x_total, mm, kk), F32),
            pltpu.VMEM((layers, rotated), F32),
            pltpu.VMEM((layers, rotated), jnp.int32),
            pltpu.VMEM((4, layers, rotated), F32),
            pltpu.SMEM((4, layers, rotated), F32),
            pltpu.SMEM((layers, 2, pairs), jnp.int32),
            pltpu.SemaphoreType.DMA((5 + zh,)),
            pltpu.SemaphoreType.DMA((5 + zh,)),
            pltpu.SemaphoreType.DMA((7,)),
            pltpu.SemaphoreType.REGULAR,
            pltpu.SemaphoreType.REGULAR,
            pltpu.SemaphoreType.REGULAR,
        ],
        compiler_params=pltpu.CompilerParams(
            collective_id=0, has_side_effects=True, vmem_limit_bytes=40 * 2**20
        ),
    )(*(
        pltpu.with_memory_space_constraint(value, pltpu.HBM)
        for value in (
            amplitudes.reshape(x_total, mm, kk),
            angles,
            hadamard,
            jnp.transpose(cz_pairs, (0, 2, 1)),
        )
    ))
    return result.reshape(1, 1, count_a, mm, kk)


def solution(mesh):
    return jax.shard_map(
        per_device,
        mesh=mesh,
        in_specs=(P("qa", "qb", None, None, None), P(), P(), P()),
        out_specs=P("qa", "qb", None, None, None),
        check_vma=False,
    )
```

```python
import functools
import math

import jax
import jax.numpy as jnp
from jax import lax
from jax.experimental import pallas as pl
from jax.experimental.pallas import tpu as pltpu
from jax.sharding import PartitionSpec as P

MESH = pl.DeviceIdType.MESH
F32 = jnp.float32
BF16 = jnp.bfloat16

Z_HALVES = 2
X_CHIPS = 4


def gate_entries(angle, flag):
    cos_part, sin_part = jnp.cos(angle), jnp.sin(angle)
    weight = flag.astype(F32)
    root = math.sqrt(0.5)
    stay, mix, turn = 1.0 - weight + weight * root, weight * root, 1.0 - weight - weight * root
    return (
        cos_part * stay - sin_part * mix,
        cos_part * mix - sin_part * turn,
        sin_part * stay + cos_part * mix,
        sin_part * mix + cos_part * turn,
    )


def split(value):
    high = value.astype(BF16)
    return high, (value - high.astype(F32)).astype(BF16)


def dot3(left, right):
    dot = functools.partial(jnp.dot, preferred_element_type=F32)
    return dot(left[0], right[0]) + (dot(left[0], right[1]) + dot(left[1], right[0]))


def log2(value):
    return value.bit_length() - 1


def kernel(
    sizes,
    amp_in, angles_in, flags_in, pairs_in, out,
    send_z, recv_z, send_p, recv_p, send_b, recv_b,
    gk, gm, gm_end, gab, sign_mid, sign_end, mid,
    amp, angles, flags, entries, gates, pairs, send_sem, recv_sem, load_sem, go_z, runs_sem, go_p,
):
    zh, zl, xc, yc, halves, ex, kk = sizes
    nz, np_, nb, na = zh * zl, xc * yc, xc * zl, zh * yc
    mm = halves * zl * ex * xc
    nab = na * nb
    bits_a, bits_b, bits_x, bits_m, bits_k = log2(na), log2(nb), log2(na), log2(mm), log2(kk)
    qubits = bits_a + bits_b + bits_x + bits_m + bits_k
    shift_m = bits_k
    shift_x = shift_m + bits_m
    shift_b = shift_x + bits_x
    shift_a = shift_b + bits_b
    rot_m = bits_a + bits_b
    rot_k = rot_m + bits_m
    sub = ex * xc
    together = 4
    steps = yc // together if yc > together else 1
    together = yc // steps

    me_a, me_b = lax.axis_index("qa"), lax.axis_index("qb")
    my_zh, my_yc = lax.div(me_a, yc), lax.rem(me_a, yc)
    my_x, my_zl = lax.div(me_b, zl), lax.rem(me_b, zl)
    my_z = my_zh * zl + my_zl
    my_p = my_x * yc + my_yc

    def at_z(other, step):
        z_half = lax.rem(my_zh + other, zh)
        z_low = lax.rem(my_zl + zl - step, zl)
        return z_half * zl + z_low, (z_half * yc + my_yc, my_x * zl + z_low)

    def at_p(step):
        p = lax.rem(my_p + 5 * step, np_)
        return p, (my_zh * yc + lax.rem(p, yc), lax.div(p, yc) * zl + my_zl)

    run = zl // 2

    def at_b(other, step):
        side = lax.rem(lax.div(my_zl, run) + other, 2)
        place = side * run + lax.rem(my_zl + step, run)
        b = lax.rem(my_x + lax.div(step, run), xc) * zl + place
        return b, (me_a, b)

    barrier = pltpu.get_barrier_semaphore()

    def signal(device, semaphore=barrier):
        pl.semaphore_signal(semaphore, inc=1, device_id=device, device_id_type=MESH)

    def to_p(semaphore):
        pl.loop(1, np_)(lambda step: signal(at_p(step)[1], semaphore))

    def to_other_run(semaphore):
        pl.loop(0, zl)(lambda step: signal(at_z(1, step)[1], semaphore))

    second = my_zh == 1
    pl.loop(1, zl)(lambda step: signal(at_z(0, step)[1]))
    pl.when(jnp.logical_not(second))(lambda: to_other_run(barrier))
    pl.when(second)(lambda: to_p(barrier))

    def load(number, source, target):
        return pltpu.make_async_copy(source, target, load_sem.at[number])

    small = [load(0, angles_in, angles), load(1, flags_in, flags), load(2, pairs_in, pairs)]
    for copy in small:
        copy.start()

    def amp_part(number):
        z_half = number // steps
        first = z_half * yc + number % steps * together
        part = pl.ds(first, together)
        return z_half, first, load(3 + number, amp_in.at[part], amp.at[part])

    for number in range(zh * steps):
        amp_part(number)[2].start()

    small[0].wait()
    small[1].wait()
    for number, value in enumerate(gate_entries(angles[...], flags[...])):
        entries[number] = value
    to_scalars = load(0, entries, gates)
    to_scalars.start()
    small[2].wait()
    to_scalars.wait()

    def entry(layer, qubit, out_one, in_one):
        value = lambda number: gates[number, layer, qubit]
        return jnp.where(
            out_one,
            jnp.where(in_one, value(3), value(2)),
            jnp.where(in_one, value(1), value(0)),
        )

    def matrix(layer, out_index, in_index, qubits_and_bits):
        result = None
        for qubit, out_bit, in_bit in qubits_and_bits:
            factor = entry(
                layer, qubit, (out_index & (1 << out_bit)) != 0, (in_index & (1 << in_bit)) != 0
            )
            result = factor if result is None else result * factor
        return result

    def signs(layer, index):
        odd = jnp.zeros(index.shape, jnp.int32)
        for pair in range(pairs.shape[2]):
            mask = jnp.left_shift(1, qubits - 1 - pairs[layer, 0, pair]) | jnp.left_shift(
                1, qubits - 1 - pairs[layer, 1, pair]
            )
            odd = odd ^ jnp.where((index & mask) == mask, 1, 0)
        return 1.0 - 2.0 * odd.astype(F32)

    def build_k(layer):
        rows = lax.broadcasted_iota(jnp.int32, (kk, kk), 0)
        cols = lax.broadcasted_iota(jnp.int32, (kk, kk), 1)
        bits = [(rot_k + n, bits_k - 1 - n, bits_k - 1 - n) for n in range(bits_k)]
        gk[layer, 0], gk[layer, 1] = split(matrix(layer, cols, rows, bits))

    bits_zl, bits_xc, bits_ex, bits_h = log2(zl), log2(xc), log2(ex), log2(halves)

    natural = [bits_m - 1 - n for n in range(bits_m)]

    def build_m():
        rows = lax.broadcasted_iota(jnp.int32, (mm, mm), 0)
        cols = lax.broadcasted_iota(jnp.int32, (mm, mm), 1)
        bits = [(rot_m + n, natural[n], natural[n]) for n in range(bits_m)]
        gm[0], gm[1] = split(matrix(0, rows, cols, bits))

    def build_m_end():
        columns = mm // halves
        rows = lax.broadcasted_iota(jnp.int32, (mm, columns), 0)
        in_bits = (
            natural[:bits_h]
            + [bits_zl - 1 - n for n in range(bits_zl)]
            + [bits_zl + bits_xc + bits_ex - 1 - n for n in range(bits_ex)]
            + [bits_zl + bits_xc - 1 - n for n in range(bits_xc)]
        )
        bits = [(rot_m + n, natural[n], in_bits[n]) for n in range(bits_m)]
        for half in range(halves):
            cols = lax.broadcasted_iota(jnp.int32, (mm, columns), 1) + half * columns
            gm_end[half, 0], gm_end[half, 1] = split(matrix(1, rows, cols, bits))

    bits_yc, bits_zh = log2(yc), log2(zh)

    def mid_bits():
        a_bits = [bits_zl + bits_zh - 1 - n for n in range(bits_zh)]
        a_bits += [bits_zl + bits_zh + bits_yc - 1 - n for n in range(bits_yc)]
        b_bits = [bits_zl + bits_zh + bits_yc + bits_xc - 1 - n for n in range(bits_xc)]
        b_bits += [bits_zl - 1 - n for n in range(bits_zl)]
        return a_bits + b_bits

    tile = min(nab, 64)

    def build_ab(layer):
        mids = mid_bits()
        if layer == 0:
            outs = mids
        else:
            outs = [bits_a - 1 - n for n in range(bits_a)]
            outs += [bits_a + bits_b - 1 - n for n in range(bits_b)]
        bits = [(n, outs[n], mids[n]) for n in range(bits_a + bits_b)]

        @pl.loop(0, nab // tile)
        def _(step):
            start = pl.multiple_of(step * tile, tile)
            rows = lax.broadcasted_iota(jnp.int32, (tile, nab), 0) + start
            cols = lax.broadcasted_iota(jnp.int32, (tile, nab), 1)
            high, low = split(matrix(layer, rows, cols, bits))
            gab[layer, 0, pl.ds(start, tile), :] = high
            gab[layer, 1, pl.ds(start, tile), :] = low

    sign_tile = min(nab, 128)

    def build_sign_mid():
        mids = mid_bits()
        per = nab // sign_tile

        @pl.loop(0, halves * ex * per)
        def _(step):
            part, start = lax.div(step, per), pl.multiple_of(lax.rem(step, per) * sign_tile, sign_tile)
            half, extra = lax.div(part, ex), lax.rem(part, ex)
            rows = lax.broadcasted_iota(jnp.int32, (sign_tile, kk), 0) + start
            cols = lax.broadcasted_iota(jnp.int32, (sign_tile, kk), 1)
            index = cols
            for n in range(bits_a + bits_b):
                index = index | (((rows >> mids[n]) & 1) << (qubits - 1 - n))
            m = ((half * zl + my_zl) * ex + extra) * xc + my_x
            index = index + (m * (1 << shift_m) + me_a * (1 << shift_x))
            sign_mid[half, pl.ds(start, sign_tile), pl.ds(pl.multiple_of(extra * kk, kk), kk)] = signs(0, index)

    def build_sign_end():
        @pl.loop(0, na)
        def _(a):
            rows = lax.broadcasted_iota(jnp.int32, (mm, kk), 0)
            cols = lax.broadcasted_iota(jnp.int32, (mm, kk), 1)
            index = cols + rows * (1 << shift_m)
            index = index + (me_a * (1 << shift_x) + me_b * (1 << shift_b) + a * (1 << shift_a))
            sign_end[a] = signs(1, index)

    def beside(value, rows):
        parts = [value[n * rows : (n + 1) * rows] for n in range(together)]
        return jnp.concatenate(parts, axis=1)

    def layer_0(number):
        z_half, first, copy = amp_part(number)
        copy.wait()
        block = amp[pl.ds(first, together)].reshape(together * mm, kk)
        block = dot3(split(block), (gk[0, 0], gk[0, 1]))
        high, low = split(block)
        block = dot3((gm[0], gm[1]), (beside(high, mm), beside(low, mm)))
        for n in range(together):
            done = block[:, n * kk : (n + 1) * kk].reshape(halves, zl, sub, kk)
            send_z[:, pl.ds(z_half * zl, zl), number % steps * together + n] = done

    def send(source, target, sems, device):
        pltpu.make_async_remote_copy(
            src_ref=source,
            dst_ref=target,
            send_sem=send_sem.at[sems],
            recv_sem=recv_sem.at[sems],
            device_id=device,
            device_id_type=MESH,
        ).start()

    def keep(source, target, sems):
        pltpu.make_async_copy(source, target, recv_sem.at[sems]).start()

    def wait_all(target, sems):
        pltpu.make_async_copy(target, target, recv_sem.at[sems]).wait()

    def wait_sent(part, sems):
        pltpu.make_async_copy(part, part, send_sem.at[sems]).wait()

    def send_z_part(half, other):
        @pl.loop(1 - other, zl)
        def _(step):
            number, device = at_z(other, step)
            send(send_z.at[half, number], recv_z.at[half, my_z], half, device)

    def keep_z(half):
        keep(send_z.at[half, my_z], recv_z.at[half, my_z], half)

    def send_p_half(half):
        @pl.loop(1, np_)
        def _(step):
            number, device = at_p(step)
            send(send_p.at[half, number], recv_p.at[half, my_p], 2 + half, device)

        keep(send_p.at[half, my_p], recv_p.at[half, my_p], 2 + half)

    def b_part(ref, half, number, group):
        return ref.at[half, number] if half == 0 else ref.at[half, number, group]

    def b_parts(half):
        return [(0, 4)] if half == 0 else [(group, 5 + group) for group in range(zh)]

    def send_b_half(half):
        for group, sems in b_parts(half):
            @pl.loop(1, nb)
            def _(step):
                number = lax.rem(me_b + step, nb)
                send(b_part(send_b, half, number, group), b_part(recv_b, half, me_b, group), sems, (me_a, number))

            keep(b_part(send_b, half, me_b, group), b_part(recv_b, half, me_b, group), sems)

    build_k(0)
    build_m()
    for number in range(steps):
        layer_0(number)
    pl.semaphore_wait(barrier, zl - 1 + my_zh * (zl + np_ - 1))
    pl.when(second)(lambda: to_other_run(go_z))
    send_z_part(0, my_zh)
    pl.when(second)(lambda: to_p(runs_sem))
    for number in range(steps, zh * steps):
        layer_0(number)

    @pl.when(jnp.logical_not(second))
    def _():
        build_ab(0)
        pl.semaphore_wait(go_z, zl)

    send_z_part(0, 1 - my_zh)
    keep_z(0)
    send_z_part(1, my_zh)
    send_z_part(1, 1 - my_zh)
    keep_z(1)

    @pl.when(second)
    def _():
        pl.semaphore_wait(runs_sem, np_ - 1)
        signal(at_z(1, 0)[1], go_p)

    pl.when(second)(lambda: build_ab(0))
    build_ab(1)
    build_sign_mid()
    mid_tile = min(nab, 128)

    def middle(half):
        wait_all(recv_z.at[half], half)

        @pl.loop(0, yc)
        def _(xr):
            for z_half in range(zh):
                for low in range(sub):
                    rows = recv_z[half, pl.ds(z_half * zl, zl), xr, low, :]
                    extra, x = low // xc, low % xc
                    send_p[half, x * yc + xr, pl.ds((extra * zh + z_half) * zl, zl), :] = rows

        if half == 0:
            @pl.when(jnp.logical_not(second))
            def _():
                pl.semaphore_wait(go_p, 1)

        send_p_half(half)
        wait_all(recv_p.at[half], 2 + half)
        parts = []
        for extra in range(ex):
            part = recv_p[half, :, pl.ds(extra * zh * zl, zh * zl), :]
            parts.append(part.reshape(nab, kk))
        high, low = split(jnp.concatenate(parts, axis=1))
        mid[0, 0] = high
        mid[0, 1] = low

        @pl.loop(0, nab // mid_tile)
        def _(step):
            start = pl.multiple_of(step * mid_tile, mid_tile)
            left = (gab[0, 0, pl.ds(start, mid_tile), :], gab[0, 1, pl.ds(start, mid_tile), :])
            value = dot3(left, (mid[0, 0], mid[0, 1])) * sign_mid[half, pl.ds(start, mid_tile), :]
            high, low = split(value)
            mid[1, 0, pl.ds(start, mid_tile), :] = high
            mid[1, 1, pl.ds(start, mid_tile), :] = low

        @pl.loop(0, nab // mid_tile)
        def _(step):
            start = pl.multiple_of(step * mid_tile, mid_tile)
            left = (gab[1, 0, pl.ds(start, mid_tile), :], gab[1, 1, pl.ds(start, mid_tile), :])
            value = dot3(left, (mid[1, 0], mid[1, 1]))
            places = mid_tile // na
            for extra in range(ex):
                part = value[:, extra * kk : (extra + 1) * kk].reshape(places, zh, yc, kk)
                send_b[half, pl.ds(step * places, places), :, pl.ds(extra * yc, yc), :] = part

        send_b_half(half)

    def last_layer(half, group):
        @pl.loop(0, steps, unroll=True)
        def _(step):
            parts = []
            for n in range(together):
                for extra in range(ex):
                    for x in range(xc):
                        row = extra * yc + step * together + n
                        parts.append(recv_b[half, pl.ds(x * zl, zl), group, row, :])
            block = jnp.concatenate(parts, axis=0)
            block = dot3(split(block), (gk[1, 0], gk[1, 1]))
            high, low = split(block)
            rows = mm // halves
            block = dot3((gm_end[half, 0], gm_end[half, 1]), (beside(high, rows), beside(low, rows)))
            for n in range(together):
                a = group * yc + step * together + n
                value = block[:, n * kk : (n + 1) * kk]
                out[a] = value if half == 0 else (out[a] + value) * sign_end[a]

    for half in range(halves):
        middle(half)
    build_k(1)
    build_m_end()
    build_sign_end()
    wait_all(recv_b.at[0], 4)
    for group in range(zh):
        last_layer(0, group)
    for group, sems in b_parts(1):
        wait_all(recv_b.at[1, :, group], sems)
        last_layer(1, group)

    for half in range(halves):
        wait_sent(send_z.at[half, pl.ds(0, nz - 1)], half)
        wait_sent(send_p.at[half, pl.ds(0, np_ - 1)], 2 + half)
    wait_sent(send_b.at[0, pl.ds(0, nb - 1)], 4)
    for group, sems in b_parts(1):
        wait_sent(send_b.at[1, pl.ds(0, nb - 1), group], sems)


def per_device(amplitudes, angles, hadamard, cz_pairs):
    count_a, count_b = lax.axis_size("qa"), lax.axis_size("qb")
    x_total, mm, kk = amplitudes.shape[2:]
    zh, xc = Z_HALVES, X_CHIPS
    yc, zl = count_a // zh, count_b // xc
    halves = 2
    ex = mm // (halves * zl * xc)
    sizes = (zh, zl, xc, yc, halves, ex, kk)
    nab = count_a * count_b
    layers, rotated = angles.shape
    pairs = cz_pairs.shape[1]
    shape_z = (halves, zh * zl, yc, ex * xc, kk)
    shape_p = (halves, xc * yc, ex * zh * zl, kk)
    shape_b = (halves, xc * zl, zh, ex * yc, kk)
    result = pl.pallas_call(
        functools.partial(kernel, sizes),
        out_shape=jax.ShapeDtypeStruct((count_a, mm, kk), F32),
        in_specs=[pl.BlockSpec(memory_space=pltpu.HBM)] * 4,
        out_specs=pl.BlockSpec(memory_space=pltpu.VMEM),
        scratch_shapes=[
            pltpu.VMEM(shape_z, F32),
            pltpu.VMEM(shape_z, F32),
            pltpu.VMEM(shape_p, F32),
            pltpu.VMEM(shape_p, F32),
            pltpu.VMEM(shape_b, F32),
            pltpu.VMEM(shape_b, F32),
            pltpu.VMEM((2, 2, kk, kk), BF16),
            pltpu.VMEM((2, mm, mm), BF16),
            pltpu.VMEM((halves, 2, mm, mm // halves), BF16),
            pltpu.VMEM((2, 2, nab, nab), BF16),
            pltpu.VMEM((halves, nab, ex * kk), F32),
            pltpu.VMEM((count_a, mm, kk), F32),
            pltpu.VMEM((2, 2, nab, ex * kk), BF16),
            pltpu.VMEM((x_total, mm, kk), F32),
            pltpu.VMEM((layers, rotated), F32),
            pltpu.VMEM((layers, rotated), jnp.int32),
            pltpu.VMEM((4, layers, rotated), F32),
            pltpu.SMEM((4, layers, rotated), F32),
            pltpu.SMEM((layers, 2, pairs), jnp.int32),
            pltpu.SemaphoreType.DMA((5 + zh,)),
            pltpu.SemaphoreType.DMA((5 + zh,)),
            pltpu.SemaphoreType.DMA((7,)),
            pltpu.SemaphoreType.REGULAR,
            pltpu.SemaphoreType.REGULAR,
            pltpu.SemaphoreType.REGULAR,
        ],
        compiler_params=pltpu.CompilerParams(
            collective_id=0, has_side_effects=True, vmem_limit_bytes=40 * 2**20
        ),
    )(*(
        pltpu.with_memory_space_constraint(value, pltpu.HBM)
        for value in (
            amplitudes.reshape(x_total, mm, kk),
            angles,
            hadamard,
            jnp.transpose(cz_pairs, (0, 2, 1)),
        )
    ))
    return result.reshape(1, 1, count_a, mm, kk)


def solution(mesh):
    return jax.shard_map(
        per_device,
        mesh=mesh,
        in_specs=(P("qa", "qb", None, None, None), P(), P(), P()),
        out_specs=P("qa", "qb", None, None, None),
        check_vma=False,
    )
```

```python
import functools
import math

import jax
import jax.numpy as jnp
from jax import lax
from jax.experimental import pallas as pl
from jax.experimental.pallas import tpu as pltpu
from jax.sharding import PartitionSpec as P

MESH = pl.DeviceIdType.MESH
F32 = jnp.float32
BF16 = jnp.bfloat16

Z_HALVES = 2
X_CHIPS = 4


def gate_entries(angle, flag):
    cos_part, sin_part = jnp.cos(angle), jnp.sin(angle)
    weight = flag.astype(F32)
    root = math.sqrt(0.5)
    stay, mix, turn = 1.0 - weight + weight * root, weight * root, 1.0 - weight - weight * root
    return (
        cos_part * stay - sin_part * mix,
        cos_part * mix - sin_part * turn,
        sin_part * stay + cos_part * mix,
        sin_part * mix + cos_part * turn,
    )


def split(value):
    high = value.astype(BF16)
    return high, (value - high.astype(F32)).astype(BF16)


def dot3(left, right):
    dot = functools.partial(jnp.dot, preferred_element_type=F32)
    return dot(left[0], right[0]) + (dot(left[0], right[1]) + dot(left[1], right[0]))


def log2(value):
    return value.bit_length() - 1


def kernel(
    sizes,
    amp_in, angles_in, flags_in, pairs_in, out,
    send_z, recv_z, send_p, recv_p, send_b, recv_b,
    gk, gm, gm_end, gab, sign_mid, sign_end, mid,
    amp, angles, flags, entries, gates, pairs, send_sem, recv_sem, load_sem, go_z, runs_sem, go_p,
):
    zh, zl, xc, yc, halves, ex, kk = sizes
    nz, np_, nb, na = zh * zl, xc * yc, xc * zl, zh * yc
    mm = halves * zl * ex * xc
    nab = na * nb
    bits_a, bits_b, bits_x, bits_m, bits_k = log2(na), log2(nb), log2(na), log2(mm), log2(kk)
    qubits = bits_a + bits_b + bits_x + bits_m + bits_k
    shift_m = bits_k
    shift_x = shift_m + bits_m
    shift_b = shift_x + bits_x
    shift_a = shift_b + bits_b
    rot_m = bits_a + bits_b
    rot_k = rot_m + bits_m
    sub = ex * xc
    together = 4
    steps = yc // together if yc > together else 1
    together = yc // steps

    me_a, me_b = lax.axis_index("qa"), lax.axis_index("qb")
    my_zh, my_yc = lax.div(me_a, yc), lax.rem(me_a, yc)
    my_x, my_zl = lax.div(me_b, zl), lax.rem(me_b, zl)
    my_z = my_zh * zl + my_zl
    my_p = my_x * yc + my_yc

    def at_z(other, step):
        z_half = lax.rem(my_zh + other, zh)
        z_low = lax.rem(my_zl + zl - step, zl)
        return z_half * zl + z_low, (z_half * yc + my_yc, my_x * zl + z_low)

    def at_p(step):
        p = lax.rem(my_p + 5 * step, np_)
        return p, (my_zh * yc + lax.rem(p, yc), lax.div(p, yc) * zl + my_zl)

    run = zl // 2

    def at_b(other, step):
        side = lax.rem(lax.div(my_zl, run) + other, 2)
        place = side * run + lax.rem(my_zl + step, run)
        b = lax.rem(my_x + lax.div(step, run), xc) * zl + place
        return b, (me_a, b)

    barrier = pltpu.get_barrier_semaphore()

    def signal(device, semaphore=barrier):
        pl.semaphore_signal(semaphore, inc=1, device_id=device, device_id_type=MESH)

    def to_p(semaphore):
        pl.loop(1, np_)(lambda step: signal(at_p(step)[1], semaphore))

    def to_other_run(semaphore):
        pl.loop(0, zl)(lambda step: signal(at_z(1, step)[1], semaphore))

    second = my_zh == 1
    pl.loop(1, zl)(lambda step: signal(at_z(0, step)[1]))
    pl.when(jnp.logical_not(second))(lambda: to_other_run(barrier))
    pl.when(second)(lambda: to_p(barrier))

    def load(number, source, target):
        return pltpu.make_async_copy(source, target, load_sem.at[number])

    small = [load(0, angles_in, angles), load(1, flags_in, flags), load(2, pairs_in, pairs)]
    for copy in small:
        copy.start()

    def amp_part(number):
        z_half = number // steps
        first = z_half * yc + number % steps * together
        part = pl.ds(first, together)
        return z_half, first, load(3 + number, amp_in.at[part], amp.at[part])

    for number in range(zh * steps):
        amp_part(number)[2].start()

    small[0].wait()
    small[1].wait()
    for number, value in enumerate(gate_entries(angles[...], flags[...])):
        entries[number] = value
    to_scalars = load(0, entries, gates)
    to_scalars.start()
    small[2].wait()
    to_scalars.wait()

    def entry(layer, qubit, out_one, in_one):
        value = lambda number: gates[number, layer, qubit]
        return jnp.where(
            out_one,
            jnp.where(in_one, value(3), value(2)),
            jnp.where(in_one, value(1), value(0)),
        )

    def matrix(layer, out_index, in_index, qubits_and_bits):
        result = None
        for qubit, out_bit, in_bit in qubits_and_bits:
            factor = entry(
                layer, qubit, (out_index & (1 << out_bit)) != 0, (in_index & (1 << in_bit)) != 0
            )
            result = factor if result is None else result * factor
        return result

    def signs(layer, index):
        odd = jnp.zeros(index.shape, jnp.int32)
        for pair in range(pairs.shape[2]):
            mask = jnp.left_shift(1, qubits - 1 - pairs[layer, 0, pair]) | jnp.left_shift(
                1, qubits - 1 - pairs[layer, 1, pair]
            )
            odd = odd ^ jnp.where((index & mask) == mask, 1, 0)
        return 1.0 - 2.0 * odd.astype(F32)

    def build_k(layer):
        rows = lax.broadcasted_iota(jnp.int32, (kk, kk), 0)
        cols = lax.broadcasted_iota(jnp.int32, (kk, kk), 1)
        bits = [(rot_k + n, bits_k - 1 - n, bits_k - 1 - n) for n in range(bits_k)]
        gk[layer, 0], gk[layer, 1] = split(matrix(layer, cols, rows, bits))

    bits_zl, bits_xc, bits_ex, bits_h = log2(zl), log2(xc), log2(ex), log2(halves)

    natural = [bits_m - 1 - n for n in range(bits_m)]

    def build_m():
        rows = lax.broadcasted_iota(jnp.int32, (mm, mm), 0)
        cols = lax.broadcasted_iota(jnp.int32, (mm, mm), 1)
        bits = [(rot_m + n, natural[n], natural[n]) for n in range(bits_m)]
        gm[0], gm[1] = split(matrix(0, rows, cols, bits))

    def build_m_end():
        columns = mm // halves
        rows = lax.broadcasted_iota(jnp.int32, (mm, columns), 0)
        in_bits = (
            natural[:bits_h]
            + [bits_zl - 1 - n for n in range(bits_zl)]
            + [bits_zl + bits_xc + bits_ex - 1 - n for n in range(bits_ex)]
            + [bits_zl + bits_xc - 1 - n for n in range(bits_xc)]
        )
        bits = [(rot_m + n, natural[n], in_bits[n]) for n in range(bits_m)]
        for half in range(halves):
            cols = lax.broadcasted_iota(jnp.int32, (mm, columns), 1) + half * columns
            gm_end[half, 0], gm_end[half, 1] = split(matrix(1, rows, cols, bits))

    bits_yc, bits_zh = log2(yc), log2(zh)

    def mid_bits():
        a_bits = [bits_zl + bits_zh - 1 - n for n in range(bits_zh)]
        a_bits += [bits_zl + bits_zh + bits_yc - 1 - n for n in range(bits_yc)]
        b_bits = [bits_zl + bits_zh + bits_yc + bits_xc - 1 - n for n in range(bits_xc)]
        b_bits += [bits_zl - 1 - n for n in range(bits_zl)]
        return a_bits + b_bits

    tile = min(nab, 64)

    def build_ab(layer):
        mids = mid_bits()
        if layer == 0:
            outs = mids
        else:
            outs = [bits_a - 1 - n for n in range(bits_a)]
            outs += [bits_a + bits_b - 1 - n for n in range(bits_b)]
        bits = [(n, outs[n], mids[n]) for n in range(bits_a + bits_b)]

        @pl.loop(0, nab // tile)
        def _(step):
            start = pl.multiple_of(step * tile, tile)
            rows = lax.broadcasted_iota(jnp.int32, (tile, nab), 0) + start
            cols = lax.broadcasted_iota(jnp.int32, (tile, nab), 1)
            high, low = split(matrix(layer, rows, cols, bits))
            gab[layer, 0, pl.ds(start, tile), :] = high
            gab[layer, 1, pl.ds(start, tile), :] = low

    sign_tile = min(nab, 128)

    def build_sign_mid():
        mids = mid_bits()
        per = nab // sign_tile

        @pl.loop(0, halves * ex * per)
        def _(step):
            part, start = lax.div(step, per), pl.multiple_of(lax.rem(step, per) * sign_tile, sign_tile)
            half, extra = lax.div(part, ex), lax.rem(part, ex)
            rows = lax.broadcasted_iota(jnp.int32, (sign_tile, kk), 0) + start
            cols = lax.broadcasted_iota(jnp.int32, (sign_tile, kk), 1)
            index = cols
            for n in range(bits_a + bits_b):
                index = index | (((rows >> mids[n]) & 1) << (qubits - 1 - n))
            m = ((half * zl + my_zl) * ex + extra) * xc + my_x
            index = index + (m * (1 << shift_m) + me_a * (1 << shift_x))
            sign_mid[half, pl.ds(start, sign_tile), pl.ds(pl.multiple_of(extra * kk, kk), kk)] = signs(0, index)

    def build_sign_end():
        @pl.loop(0, na)
        def _(a):
            rows = lax.broadcasted_iota(jnp.int32, (mm, kk), 0)
            cols = lax.broadcasted_iota(jnp.int32, (mm, kk), 1)
            index = cols + rows * (1 << shift_m)
            index = index + (me_a * (1 << shift_x) + me_b * (1 << shift_b) + a * (1 << shift_a))
            sign_end[a] = signs(1, index)

    def beside(value, rows):
        parts = [value[n * rows : (n + 1) * rows] for n in range(together)]
        return jnp.concatenate(parts, axis=1)

    def layer_0(number):
        z_half, first, copy = amp_part(number)
        copy.wait()
        block = amp[pl.ds(first, together)].reshape(together * mm, kk)
        block = dot3(split(block), (gk[0, 0], gk[0, 1]))
        high, low = split(block)
        block = dot3((gm[0], gm[1]), (beside(high, mm), beside(low, mm)))
        for n in range(together):
            done = block[:, n * kk : (n + 1) * kk].reshape(halves, zl, sub, kk)
            send_z[:, pl.ds(z_half * zl, zl), number % steps * together + n] = done

    def send(source, target, sems, device):
        pltpu.make_async_remote_copy(
            src_ref=source,
            dst_ref=target,
            send_sem=send_sem.at[sems],
            recv_sem=recv_sem.at[sems],
            device_id=device,
            device_id_type=MESH,
        ).start()

    def keep(source, target, sems):
        pltpu.make_async_copy(source, target, recv_sem.at[sems]).start()

    def wait_all(target, sems):
        pltpu.make_async_copy(target, target, recv_sem.at[sems]).wait()

    def wait_sent(part, sems):
        pltpu.make_async_copy(part, part, send_sem.at[sems]).wait()

    def send_z_part(half, other):
        @pl.loop(1 - other, zl)
        def _(step):
            number, device = at_z(other, step)
            send(send_z.at[half, number], recv_z.at[half, my_z], half, device)

    def keep_z(half):
        keep(send_z.at[half, my_z], recv_z.at[half, my_z], half)

    def send_p_half(half):
        @pl.loop(1, np_)
        def _(step):
            number, device = at_p(step)
            send(send_p.at[half, number], recv_p.at[half, my_p], 2 + half, device)

        keep(send_p.at[half, my_p], recv_p.at[half, my_p], 2 + half)

    def b_part(ref, half, number, group):
        return ref.at[half, number] if half == 0 else ref.at[half, number, group]

    def b_parts(half):
        return [(0, 4)] if half == 0 else [(group, 5 + group) for group in range(zh)]

    def send_b_half(half):
        for group, sems in b_parts(half):
            @pl.loop(1, nb)
            def _(step):
                number = lax.rem(me_b + step, nb)
                send(b_part(send_b, half, number, group), b_part(recv_b, half, me_b, group), sems, (me_a, number))

            keep(b_part(send_b, half, me_b, group), b_part(recv_b, half, me_b, group), sems)

    build_k(0)
    build_m()
    for number in range(steps):
        layer_0(number)
    pl.semaphore_wait(barrier, zl - 1 + my_zh * (zl + np_ - 1))
    pl.when(second)(lambda: to_other_run(go_z))
    send_z_part(0, my_zh)
    pl.when(second)(lambda: to_p(runs_sem))
    for number in range(steps, zh * steps):
        layer_0(number)

    @pl.when(jnp.logical_not(second))
    def _():
        build_ab(0)
        pl.semaphore_wait(go_z, zl)

    send_z_part(0, 1 - my_zh)
    keep_z(0)
    send_z_part(1, my_zh)
    send_z_part(1, 1 - my_zh)
    keep_z(1)

    @pl.when(second)
    def _():
        pl.semaphore_wait(runs_sem, np_ - 1)
        signal(at_z(1, 0)[1], go_p)

    pl.when(second)(lambda: build_ab(0))
    build_ab(1)
    build_sign_mid()
    mid_tile = min(nab, 128)

    def middle(half):
        wait_all(recv_z.at[half], half)

        @pl.loop(0, yc)
        def _(xr):
            for z_half in range(zh):
                for low in range(sub):
                    rows = recv_z[half, pl.ds(z_half * zl, zl), xr, low, :]
                    extra, x = low // xc, low % xc
                    send_p[half, x * yc + xr, pl.ds((extra * zh + z_half) * zl, zl), :] = rows

        if half == 0:
            @pl.when(jnp.logical_not(second))
            def _():
                pl.semaphore_wait(go_p, 1)

        send_p_half(half)
        wait_all(recv_p.at[half], 2 + half)
        parts = []
        for extra in range(ex):
            part = recv_p[half, :, pl.ds(extra * zh * zl, zh * zl), :]
            parts.append(part.reshape(nab, kk))
        high, low = split(jnp.concatenate(parts, axis=1))
        mid[0, 0] = high
        mid[0, 1] = low

        @pl.loop(0, nab // mid_tile)
        def _(step):
            start = pl.multiple_of(step * mid_tile, mid_tile)
            left = (gab[0, 0, pl.ds(start, mid_tile), :], gab[0, 1, pl.ds(start, mid_tile), :])
            value = dot3(left, (mid[0, 0], mid[0, 1])) * sign_mid[half, pl.ds(start, mid_tile), :]
            high, low = split(value)
            mid[1, 0, pl.ds(start, mid_tile), :] = high
            mid[1, 1, pl.ds(start, mid_tile), :] = low

        @pl.loop(0, nab // mid_tile)
        def _(step):
            start = pl.multiple_of(step * mid_tile, mid_tile)
            left = (gab[1, 0, pl.ds(start, mid_tile), :], gab[1, 1, pl.ds(start, mid_tile), :])
            value = dot3(left, (mid[1, 0], mid[1, 1]))
            places = mid_tile // na
            for extra in range(ex):
                part = value[:, extra * kk : (extra + 1) * kk].reshape(places, zh, yc, kk)
                send_b[half, pl.ds(step * places, places), :, pl.ds(extra * yc, yc), :] = part

        send_b_half(half)

    def last_layer(half, group):
        @pl.loop(0, steps, unroll=True)
        def _(step):
            parts = []
            for n in range(together):
                for extra in range(ex):
                    for x in range(xc):
                        row = extra * yc + step * together + n
                        parts.append(recv_b[half, pl.ds(x * zl, zl), group, row, :])
            block = jnp.concatenate(parts, axis=0)
            block = dot3(split(block), (gk[1, 0], gk[1, 1]))
            high, low = split(block)
            rows = mm // halves
            block = dot3((gm_end[half, 0], gm_end[half, 1]), (beside(high, rows), beside(low, rows)))
            for n in range(together):
                a = group * yc + step * together + n
                value = block[:, n * kk : (n + 1) * kk]
                out[a] = value if half == 0 else (out[a] + value) * sign_end[a]

    for half in range(halves):
        middle(half)
    build_k(1)
    build_m_end()
    build_sign_end()
    wait_all(recv_b.at[0], 4)
    for group in range(zh):
        last_layer(0, group)
    for half in range(halves):
        wait_sent(send_z.at[half, pl.ds(0, nz - 1)], half)
        wait_sent(send_p.at[half, pl.ds(0, np_ - 1)], 2 + half)
    wait_sent(send_b.at[0, pl.ds(0, nb - 1)], 4)
    for group, sems in b_parts(1):
        wait_all(recv_b.at[1, :, group], sems)
        last_layer(1, group)

    for group, sems in b_parts(1):
        wait_sent(send_b.at[1, pl.ds(0, nb - 1), group], sems)


def per_device(amplitudes, angles, hadamard, cz_pairs):
    count_a, count_b = lax.axis_size("qa"), lax.axis_size("qb")
    x_total, mm, kk = amplitudes.shape[2:]
    zh, xc = Z_HALVES, X_CHIPS
    yc, zl = count_a // zh, count_b // xc
    halves = 2
    ex = mm // (halves * zl * xc)
    sizes = (zh, zl, xc, yc, halves, ex, kk)
    nab = count_a * count_b
    layers, rotated = angles.shape
    pairs = cz_pairs.shape[1]
    shape_z = (halves, zh * zl, yc, ex * xc, kk)
    shape_p = (halves, xc * yc, ex * zh * zl, kk)
    shape_b = (halves, xc * zl, zh, ex * yc, kk)
    result = pl.pallas_call(
        functools.partial(kernel, sizes),
        out_shape=jax.ShapeDtypeStruct((count_a, mm, kk), F32),
        in_specs=[pl.BlockSpec(memory_space=pltpu.HBM)] * 4,
        out_specs=pl.BlockSpec(memory_space=pltpu.VMEM),
        scratch_shapes=[
            pltpu.VMEM(shape_z, F32),
            pltpu.VMEM(shape_z, F32),
            pltpu.VMEM(shape_p, F32),
            pltpu.VMEM(shape_p, F32),
            pltpu.VMEM(shape_b, F32),
            pltpu.VMEM(shape_b, F32),
            pltpu.VMEM((2, 2, kk, kk), BF16),
            pltpu.VMEM((2, mm, mm), BF16),
            pltpu.VMEM((halves, 2, mm, mm // halves), BF16),
            pltpu.VMEM((2, 2, nab, nab), BF16),
            pltpu.VMEM((halves, nab, ex * kk), F32),
            pltpu.VMEM((count_a, mm, kk), F32),
            pltpu.VMEM((2, 2, nab, ex * kk), BF16),
            pltpu.VMEM((x_total, mm, kk), F32),
            pltpu.VMEM((layers, rotated), F32),
            pltpu.VMEM((layers, rotated), jnp.int32),
            pltpu.VMEM((4, layers, rotated), F32),
            pltpu.SMEM((4, layers, rotated), F32),
            pltpu.SMEM((layers, 2, pairs), jnp.int32),
            pltpu.SemaphoreType.DMA((5 + zh,)),
            pltpu.SemaphoreType.DMA((5 + zh,)),
            pltpu.SemaphoreType.DMA((7,)),
            pltpu.SemaphoreType.REGULAR,
            pltpu.SemaphoreType.REGULAR,
            pltpu.SemaphoreType.REGULAR,
        ],
        compiler_params=pltpu.CompilerParams(
            collective_id=0, has_side_effects=True, vmem_limit_bytes=40 * 2**20
        ),
    )(*(
        pltpu.with_memory_space_constraint(value, pltpu.HBM)
        for value in (
            amplitudes.reshape(x_total, mm, kk),
            angles,
            hadamard,
            jnp.transpose(cz_pairs, (0, 2, 1)),
        )
    ))
    return result.reshape(1, 1, count_a, mm, kk)


def solution(mesh):
    return jax.shard_map(
        per_device,
        mesh=mesh,
        in_specs=(P("qa", "qb", None, None, None), P(), P(), P()),
        out_specs=P("qa", "qb", None, None, None),
        check_vma=False,
    )
```
